512 devices in a mesh: ens: 8 (over z_hi, x), grid: 64 (over z_lo, y, core).
Axes of the slice: x: 4, y: 4, z: 16 (z_hi: 2, z_lo: 8; z = z_hi * 8 + z_lo), core: 2. Of those that a mesh axis runs over, the one named last changes fastest.
Arguments:
- latent_fields: bfloat16 [8, 16384, 1024], P('ens', 'grid'), may hold values from -6 to 6
- neighbours: int32 [8, 16384], P(None, 'grid'), may hold values from 0 to 16383, as said below
- mix_weight: bfloat16 [1024, 1024], replicated, may hold values from -0.1875 to 0.1875
- norm_gain: float32 [1024], replicated, may hold values from 0.1 to 1.9
- output_projector: bfloat16 [100, 1024], replicated, may hold values from -0.1875 to 0.1875
- verifying_fields: float32 [100, 16384], P(None, 'grid'), may hold values from -6 to 6
- area: float32 [16384], P('grid'), may hold values from 0.25 to 2.5
Outputs:
- latent_sensitivity: bfloat16 [8, 16384, 1024], P('ens', 'grid')
- loss: float32 [], replicated
The draws below stay inside these ranges and needn't reach their ends.
Inputs may be any that keep to these rules, and one draw needn't show every extreme that they name: neighbours[k, p] differs from p by at most 64.
All inputs are finite; a program needn't handle non-finite values.
Results may differ from the reference program's by a relative error of at most 0.011.
Values may be sent and summed in bfloat16 or wider, within the bound.
A program may use at most 64 MiB of HBM per device.

```python
import math
import jax
import jax.numpy as jnp
from jax import lax

C = 1024
VARS = 100
NEIGHBOURS = 8
HALO = 64
MEMBERS = 8
POINTS = 16384


def draw_neighbours(key, part):
    key = jax.random.fold_in(key, 11)
    place = jnp.arange(POINTS, dtype=jnp.int32)[None, :]
    offset = jax.random.randint(key, (NEIGHBOURS, POINTS), -HALO, HALO + 1, dtype=jnp.int32)
    return jnp.clip(place + offset, 0, POINTS - 1).astype(jnp.int32)


def block_scale(stream_key, extent, split, smallest, top_value):
    def one(dim, blocks):
        draws = jax.random.uniform(jax.random.fold_in(jax.random.fold_in(stream_key, 6), dim), (blocks,), jnp.float32, smallest / len(split), top_value / len(split))
        return jnp.repeat(jnp.exp(draws), extent[dim] // blocks).reshape((-1,) + (1,) * (len(extent) - dim - 1))

    loudness = one(*split[0])
    for cut in split[1:]:
        loudness = loudness * one(*cut)
    return loudness


def gaussian(own_key, dims, spread, bound, shards=(), kind=jnp.bfloat16):
    drawn = jax.random.normal(own_key, dims, jnp.float32) * spread
    if len(shards) > 0:
        drawn = block_scale(own_key, dims, shards, -0.22, 0.18) * drawn
    return jnp.clip(drawn, min=-bound, max=bound).astype(kind)


def setup_inputs(seed: int = 0) -> dict:
    key_of = jax.random.split(jax.random.key(seed), 8)
    latent_fields = gaussian(key_of[0], (MEMBERS, POINTS, C), 1.0, 6.0, ((0, 8), (1, 64)))
    neighbours = draw_neighbours(jax.random.fold_in(key_of[7], 71), 0)
    mix_weight = gaussian(key_of[2], (C, C), C ** -0.5, 0.1875)
    norm_gain = jnp.clip(1.0 + 0.18 * jax.random.normal(key_of[3], (C,), jnp.float32), 0.1, 1.9)
    output_projector = gaussian(key_of[4], (VARS, C), C ** -0.5, 0.1875)
    verifying_fields = gaussian(key_of[5], (VARS, POINTS), 1.0, 6.0, ((1, 64),), jnp.float32)
    area = jnp.clip(jnp.exp(math.log(2.5) - 2.3025851 * jax.random.uniform(key_of[6], (POINTS,), jnp.float32) ** block_scale(key_of[6], (POINTS,), ((0, 64),), -0.2, 0.2)), 0.25, 2.5)
    return {"latent_fields": latent_fields, "neighbours": neighbours, "mix_weight": mix_weight, "norm_gain": norm_gain, "output_projector": output_projector, "verifying_fields": verifying_fields, "area": area}


gap_square = 0.01

def aggregate(state, neighbours):
    total = jnp.zeros(state.shape, jnp.float32)
    for k in range(NEIGHBOURS):
        total = total + state[neighbours[k]].astype(jnp.float32)
    return total / NEIGHBOURS

def layer_forward(state, agg, mix_weight, norm_gain):
    mixed = state.astype(jnp.float32) + agg
    centre = mixed - lax.optimization_barrier(jnp.mean(mixed, axis=-1, keepdims=True))
    scale = lax.rsqrt(lax.optimization_barrier(jnp.mean(centre * centre, axis=-1, keepdims=True)) + 1e-05)
    unit = centre * scale
    normed = (unit * norm_gain).astype(jnp.bfloat16)
    pre = jnp.dot(normed, mix_weight, preferred_element_type=jnp.float32)
    after = (state.astype(jnp.float32) + jax.nn.gelu(pre)).astype(jnp.bfloat16)
    return (after, pre, unit, scale)

def decode(after, output_projector):
    return lax.dot_general(output_projector, after, (((1,), (1,)), ((), ())), preferred_element_type=jnp.float32)

def layer_backward(state_grad_y, pre, unit, scale, mix_weight, norm_gain):
    gelu_back = jax.vjp(jax.nn.gelu, pre)[1]
    grad_pre = gelu_back(state_grad_y)[0].astype(jnp.bfloat16)
    grad_normed = lax.dot_general(grad_pre, mix_weight, (((1,), (1,)), ((), ())), preferred_element_type=jnp.float32)
    grad_unit = grad_normed * norm_gain
    return scale * (grad_unit - lax.optimization_barrier(jnp.mean(grad_unit, axis=-1, keepdims=True)) - unit * lax.optimization_barrier(jnp.mean(grad_unit * unit, axis=-1, keepdims=True)))

def reference(latent_fields, neighbours, mix_weight, norm_gain, output_projector, verifying_fields, area):

    def block_apply(state):
        agg = aggregate(state, neighbours)
        after = layer_forward(state, agg, mix_weight, norm_gain)[0]
        return decode(after, output_projector)
    predicted_fields = lax.map(block_apply, latent_fields)
    member_count = MEMBERS
    pair_coefficient = 1.0 / (member_count * (member_count - 1))
    accuracy_component = jnp.sqrt((predicted_fields - verifying_fields[None]) ** 2 + gap_square)
    accuracy_sensitivity = (predicted_fields - verifying_fields[None]) / accuracy_component
    dispersion_component = jnp.zeros(verifying_fields.shape, jnp.float32)
    block_parameter_sensitivities = []
    for sample_position in range(member_count):
        couple_sensitivity = jnp.zeros(verifying_fields.shape, jnp.float32)
        for second_position in range(member_count):
            if second_position != sample_position:
                sample_gap = predicted_fields[sample_position] - predicted_fields[second_position]
                smooth = jnp.sqrt(sample_gap * sample_gap + gap_square)
                dispersion_component = dispersion_component + 0.5 * smooth
                couple_sensitivity = couple_sensitivity - sample_gap / smooth
        block_parameter_sensitivities.append(area[None] * (accuracy_sensitivity[sample_position] / member_count + pair_coefficient * couple_sensitivity))
    point_loss = area[None] * (lax.optimization_barrier(jnp.sum(accuracy_component, axis=0)) / member_count - pair_coefficient * dispersion_component)
    loss = jnp.sum(point_loss) / (POINTS * VARS)
    prediction_sensitivity = jnp.stack(block_parameter_sensitivities).astype(jnp.bfloat16)

    def block_reverse_sweep(pair):
        state, grad_f = pair
        agg = aggregate(state, neighbours)
        after, pre, unit, scale = layer_forward(state, agg, mix_weight, norm_gain)
        grad_y = lax.dot_general(grad_f, output_projector, (((0,), (0,)), ((), ())), preferred_element_type=jnp.float32)
        grad_mixed = layer_backward(grad_y, pre, unit, scale, mix_weight, norm_gain)
        total = grad_y + grad_mixed
        spread_back = grad_mixed / NEIGHBOURS
        for k in range(NEIGHBOURS):
            total = total.at[neighbours[k]].add(spread_back)
        return total.astype(jnp.bfloat16)
    latent_sensitivity = lax.map(block_reverse_sweep, (latent_fields, prediction_sensitivity))
    return (latent_sensitivity, loss)
```

```python
import functools

import jax
import jax.numpy as jnp
from jax import lax
from jax.experimental import pallas as pl
from jax.experimental.pallas import tpu as pltpu
from jax.sharding import PartitionSpec as P

ZH, XN, ZL, YN, CORES = 2, 4, 8, 4, 2
MESH = pl.DeviceIdType.MESH
GAP = 0.01
F32, BF16 = jnp.float32, jnp.bfloat16


def dot(a, b, ca, cb):
    return lax.dot_general(a, b, (((ca,), (cb,)), ((), ())), preferred_element_type=F32)


def device(zh, x, zl, y, core):
    return (zh * XN + x, (zl * YN + y) * CORES + core)


def kernel(
    total_points,
    x_hbm,
    nb_hbm,
    w_hbm,
    gain_hbm,
    proj_hbm,
    ver_hbm,
    area_hbm,
    out_ref,
    loss_ref,
    ext,
    w,
    pin,
    pv,
    nb,
    gain,
    ver,
    area,
    vert,
    areat,
    at_i,
    at_e,
    unit,
    scale,
    slope,
    fld,
    gs,
    direct,
    gmb,
    gsend,
    garr,
    lacc,
    lone,
    ltwo,
    in_sem,
    halo_s,
    halo_r,
    fld_s,
    fld_r,
    gh_s,
    gh_r,
    l1_s,
    l1_r,
    l2_s,
    l2_r,
):
    rows, c_dim = x_hbm.shape
    rim = rows // 4
    half = rows // 2
    vars_n = proj_hbm.shape[0]
    lanes = pv.shape[0]
    members = ZH * XN
    e, g = lax.axis_index("ens"), lax.axis_index("grid")
    bands = lax.axis_size("grid")
    zh, x = e // XN, e % XN
    zl, y, core = g // (YN * CORES), (g // CORES) % YN, g % CORES
    has_left, has_right = g > 0, g < bands - 1
    left, right = (e, g - 1), (e, g + 1)

    def at_z(d, core_):
        z = (zh * ZL + zl + d + 2 * ZH * ZL) % (ZH * ZL)
        return device(z // ZL, x, z % ZL, y, core_)

    offsets = [d for d in range(-(ZL // 2) + 1, ZL // 2 + 1) if d]
    xy = [(dx, dy) for dx in range(XN) for dy in range(YN) if (dx, dy) != (0, 0)]
    to_xy = [device(zh, (x + dx) % XN, zl, (y + dy) % YN, core) for dx, dy in xy]
    zc = [(d, dc) for d in offsets for dc in range(CORES)]
    to_zc = [at_z(d, (core + dc) % CORES) for d, dc in zc]
    from_zc = [at_z(-d, (core + dc) % CORES) for d, dc in zc]
    other_core = device(zh, x, zl, y, 1 - core)
    partner = device(1 - zh, x, zl, y, core)
    to_x = [device(zh, (x + dx) % XN, zl, y, core) for dx in range(1, XN)]

    barrier = pltpu.get_barrier_semaphore()

    def hello(to):
        pl.semaphore_signal(barrier, inc=1, device_id=to, device_id_type=MESH)

    hello(partner)
    for to in from_zc + to_xy:
        hello(to)
    pl.when(has_left)(lambda: hello(left))
    pl.when(has_right)(lambda: hello(right))

    loads = [
        pltpu.make_async_copy(nb_hbm, nb, in_sem.at[0]),
        pltpu.make_async_copy(x_hbm, ext.at[pl.ds(rim, rows)], in_sem.at[1]),
        pltpu.make_async_copy(gain_hbm, gain, in_sem.at[2]),
        pltpu.make_async_copy(w_hbm, w, in_sem.at[3]),
        pltpu.make_async_copy(proj_hbm, pin, in_sem.at[4]),
        pltpu.make_async_copy(ver_hbm, ver, in_sem.at[5]),
        pltpu.make_async_copy(area_hbm, area, in_sem.at[6]),
    ]
    for load in loads:
        load.start()

    @pl.when(jnp.logical_not(has_left))
    def _():
        ext[0:rim] = jnp.zeros((rim, c_dim), BF16)

    @pl.when(jnp.logical_not(has_right))
    def _():
        ext[rim + rows :] = jnp.zeros((rim, c_dim), BF16)

    loads[0].wait()
    near = pltpu.roll(nb[...] - (g * rows - rim), rows - rim, axis=1)

    def counts(first, size, lo):
        q = lax.broadcasted_iota(jnp.int32, (size, half), 0) + first
        total = jnp.zeros((size, half), F32)
        for k in range(nb.shape[0]):
            total = total + jnp.where(q == near[k : k + 1, lo : lo + half], 1.0, 0.0)
        return total.astype(BF16)

    at_i[...] = counts(rim, rows, 0)
    at_e[...] = counts(0, rows + 2 * rim, half)

    def forward(c, state, at, window):
        mixed = state.astype(F32) + dot(at, window, 0, 0) * (1.0 / nb.shape[0])
        centre = mixed - jnp.mean(mixed, axis=-1, keepdims=True)
        r = lax.rsqrt(jnp.mean(centre * centre, axis=-1, keepdims=True) + 1e-05)
        xh = centre * r
        here = pl.ds(c * half, half)
        unit[here] = xh
        scale[here] = jnp.broadcast_to(r, (half, scale.shape[1]))
        normed = (xh * gain[...]).astype(BF16)
        pre = dot(normed, w[...], 1, 0)
        k0 = 0.7978845608028654
        sq = pre * pre
        t = jnp.tanh(k0 * pre * (1.0 + 0.044715 * sq))
        cdf = 0.5 * (1.0 + t)
        out = (state.astype(F32) + pre * cdf).astype(BF16)
        slope[here] = cdf + 0.5 * pre * (1.0 - t * t) * (k0 * (1.0 + 3 * 0.044715 * sq))
        fld[c, e] = dot(out, pv[...], 1, 1).astype(BF16)

    loads[1].wait()
    loads[2].wait()
    loads[3].wait()
    loads[4].wait()
    pv[0 : vars_n // 16 * 16] = pin[0 : vars_n // 16 * 16]
    pv[vars_n // 16 * 16 :] = jnp.zeros((lanes - vars_n // 16 * 16, c_dim), BF16)
    pv[vars_n // 16 * 16 : vars_n] = pin[vars_n // 16 * 16 :]
    forward(0, ext[rim + rim : rim + rim + half], at_i[...], ext[rim : rim + rows])

    pl.semaphore_wait(
        barrier, 1 + len(to_zc) + len(to_xy) + has_left.astype(jnp.int32) + has_right.astype(jnp.int32)
    )

    def remote(src, dst, s_sem, r_sem, to):
        return pltpu.make_async_remote_copy(
            src_ref=src, dst_ref=dst, send_sem=s_sem, recv_sem=r_sem, device_id=to, device_id_type=MESH
        )

    halo_left = remote(
        ext.at[pl.ds(rim, rim)], ext.at[pl.ds(rim + rows, rim)], halo_s.at[0], halo_r.at[1], left
    )
    halo_right = remote(
        ext.at[pl.ds(rows, rim)], ext.at[pl.ds(0, rim)], halo_s.at[1], halo_r.at[0], right
    )
    from_left = remote(ext.at[pl.ds(0, rim)], ext.at[pl.ds(0, rim)], halo_s.at[0], halo_r.at[0], left)
    from_right = remote(
        ext.at[pl.ds(rim + rows, rim)],
        ext.at[pl.ds(rim + rows, rim)],
        halo_s.at[1],
        halo_r.at[1],
        right,
    )
    pl.when(has_left)(halo_left.start)
    pl.when(has_right)(halo_right.start)

    mate = (1 - zh) * XN + x

    def field(c, member, i, to):
        slot = fld.at[c, member]
        return remote(slot, slot, fld_s.at[c, i], fld_r.at[c, member], to)

    sent = []

    def send_own(c):
        for i, to in enumerate([partner] + to_x):
            copy = field(c, e, i, to)
            copy.start()
            sent.append(copy)

    def relay(c):
        field(c, mate, 0, partner).wait_recv()
        for i, to in enumerate(to_x):
            copy = field(c, mate, XN + i, to)
            copy.start()
            sent.append(copy)

    send_own(0)
    pl.when(has_left)(from_left.wait_recv)
    pl.when(has_right)(from_right.wait_recv)
    state_e = jnp.concatenate([ext[rows : rows + rim], ext[rim : 2 * rim]], axis=0)
    forward(1, state_e, at_e[...], ext[...])
    send_own(1)

    loads[5].wait()
    loads[6].wait()
    tall = jnp.concatenate([ver[...], jnp.zeros((lanes - vars_n, rows), F32)], axis=0)
    vert[...] = pltpu.roll(tall, rows - rim, axis=1).T
    areat[...] = pltpu.roll(jnp.broadcast_to(area[...], (lanes, rows)), rows - rim, axis=1).T
    lacc[...] = jnp.zeros(lacc.shape, F32)

    def score(c):
        step = 32

        def some(i, carry):
            at = pl.ds(pl.multiple_of(i * step, step), step)
            there = pl.ds(pl.multiple_of(c * half + i * step, step), step)
            f = [
                [fld[c, h * XN + (x + dx) % XN, at, :].astype(F32) for dx in range(XN)]
                for h in range(ZH)
            ]
            truth, weight = vert[there], areat[there]
            kept = {}
            for h in range(ZH):
                d = f[h][0] - truth
                q = d * d + GAP
                root = lax.rsqrt(q)
                good, pull = q * root, d * root
                spread = jnp.zeros_like(d)
                push = jnp.zeros_like(d)
                for dx in range(XN):
                    for h2 in range(ZH):
                        if (h2, dx) == (h, 0):
                            continue
                        if (h, h2, dx) == (1, 0, 0):
                            s, sp = kept["s"], -kept["sp"]
                        else:
                            d = f[h][0] - f[h2][dx]
                            q = d * d + GAP
                            root = lax.rsqrt(q)
                            s, sp = q * root, d * root
                        if (h, h2, dx) == (0, 1, 0):
                            kept["s"], kept["sp"] = s, sp
                        spread, push = spread + s, push + sp
                pair = 1.0 / (members * (members - 1))
                kept[h] = weight * (pull * (1.0 / members) - pair * push)
                part = weight * (good * (1.0 / members) - (0.5 * pair) * spread)
                lacc[...] += sum(part[8 * j : 8 * j + 8] for j in range(step // 8))
            gs[there] = jnp.where(zh == 0, kept[0], kept[1]).astype(BF16)
            return carry

        lax.fori_loop(0, half // step, some, 0)

    def backward(c):
        here = pl.ds(c * half, half)
        grad_y = dot(gs[here], pv[...], 1, 0)
        grad_pre = (grad_y * slope[here]).astype(BF16)
        gx = dot(grad_pre, w[...], 1, 1) * gain[...]
        xh = unit[here]
        flat = jnp.mean(gx, axis=-1, keepdims=True)
        lean = jnp.mean(gx * xh, axis=-1, keepdims=True)
        gm = scale[here][:, 0:1] * (gx - flat - xh * lean)
        direct[here] = grad_y + gm
        gmb[here] = gm.astype(BF16)

    def others(c):
        for dx in range(1, XN):
            field(c, zh * XN + (x + dx) % XN, 0, partner).wait_recv()
            field(c, (1 - zh) * XN + (x + dx) % XN, 0, partner).wait_recv()

    relay(0)
    others(0)
    score(0)
    backward(0)
    relay(1)
    others(1)
    score(1)

    lane = lax.broadcasted_iota(jnp.int32, (1, lanes), 1)
    mine1 = x * YN + y
    lone[mine1] = jnp.where(lane < vars_n, jnp.sum(lacc[...], axis=0, keepdims=True), 0.0)
    for i, to in enumerate(to_xy):
        copy = remote(lone.at[mine1], lone.at[mine1], l1_s.at[i], l1_r.at[mine1], to)
        copy.start()
        sent.append(copy)

    backward(1)
    per = 1.0 / nb.shape[0]
    gsend[0] = (dot(at_e[0:rim], gmb[half:], 1, 0) * per).astype(BF16)
    gsend[1] = (dot(at_e[rim + rows :], gmb[half:], 1, 0) * per).astype(BF16)
    grad_left = remote(gsend.at[0], garr.at[1], gh_s.at[0], gh_r.at[1], left)
    grad_right = remote(gsend.at[1], garr.at[0], gh_s.at[1], gh_r.at[0], right)
    pl.when(has_left)(grad_left.start)
    pl.when(has_right)(grad_right.start)

    for dx, dy in xy:
        slot = ((x + dx) % XN) * YN + (y + dy) % YN
        remote(lone.at[slot], lone.at[slot], l1_s.at[0], l1_r.at[slot], other_core).wait_recv()
    mine2 = zl * CORES + core
    acc = lone[0]
    for i in range(1, XN * YN):
        acc = acc + lone[i]
    ltwo[mine2] = acc
    for i, to in enumerate([other_core] + to_zc):
        copy = remote(ltwo.at[mine2], ltwo.at[mine2], l2_s.at[i], l2_r.at[mine2], to)
        copy.start()
        sent.append(copy)

    spread = (dot(at_i[...], gmb[0:half], 1, 0) + dot(at_e[rim : rim + rows], gmb[half:], 1, 0)) * per
    out_ref[rim : rim + half] = (spread[rim : rim + half] + direct[0:half]).astype(BF16)
    tail = spread[rows - rim :] + direct[half : half + rim]
    head = spread[0:rim] + direct[half + rim :]
    direct[half : half + rim] = tail
    direct[half + rim :] = head

    @pl.when(jnp.logical_not(has_left))
    def _():
        garr[0] = jnp.zeros((rim, c_dim), BF16)

    @pl.when(jnp.logical_not(has_right))
    def _():
        garr[1] = jnp.zeros((rim, c_dim), BF16)

    @pl.when(has_left)
    def _():
        remote(garr.at[0], garr.at[0], gh_s.at[0], gh_r.at[0], left).wait_recv()

    @pl.when(has_right)
    def _():
        remote(garr.at[1], garr.at[1], gh_s.at[1], gh_r.at[1], right).wait_recv()

    out_ref[0:rim] = (direct[half + rim :] + garr[0].astype(F32)).astype(BF16)
    out_ref[rows - rim :] = (direct[half : half + rim] + garr[1].astype(F32)).astype(BF16)

    for slot in range(ZL * CORES):

        @pl.when(slot != mine2)
        def _():
            remote(ltwo.at[slot], ltwo.at[slot], l2_s.at[0], l2_r.at[slot], other_core).wait_recv()

    acc = ltwo[0]
    for i in range(1, ZL * CORES):
        acc = acc + ltwo[i]
    loss_ref[0, 0] = jnp.sum(acc) * (1.0 / (total_points * vars_n))

    for copy in sent:
        copy.wait_send()
    pl.when(has_left)(halo_left.wait_send)
    pl.when(has_right)(halo_right.wait_send)
    pl.when(has_left)(grad_left.wait_send)
    pl.when(has_right)(grad_right.wait_send)


def shards(
    latent_fields, neighbours, mix_weight, norm_gain, output_projector, verifying_fields, area
):
    _, rows, c_dim = latent_fields.shape
    count = neighbours.shape[0]
    vars_n = output_projector.shape[0]
    rim, half, lanes = rows // 4, rows // 2, 128
    members = ZH * XN
    anywhere = pl.BlockSpec(memory_space=pl.ANY)
    dma = pltpu.SemaphoreType.DMA
    n_xy, n_zc = XN * YN, ZL * CORES
    out, loss = pl.pallas_call(
        functools.partial(kernel, rows * lax.axis_size("grid")),
        out_shape=(
            jax.ShapeDtypeStruct((rows, c_dim), BF16),
            jax.ShapeDtypeStruct((1, 1), F32),
        ),
        in_specs=[anywhere] * 7,
        out_specs=(
            pl.BlockSpec(memory_space=pltpu.VMEM),
            pl.BlockSpec(memory_space=pltpu.SMEM),
        ),
        scratch_shapes=[
            pltpu.VMEM((rows + 2 * rim, c_dim), BF16),
            pltpu.VMEM(mix_weight.shape, BF16),
            pltpu.VMEM((vars_n, c_dim), BF16),
            pltpu.VMEM((lanes, c_dim), BF16),
            pltpu.VMEM((count, rows), jnp.int32),
            pltpu.VMEM((1, c_dim), F32),
            pltpu.VMEM((vars_n, rows), F32),
            pltpu.VMEM((1, rows), F32),
            pltpu.VMEM((rows, lanes), F32),
            pltpu.VMEM((rows, lanes), F32),
            pltpu.VMEM((rows, half), BF16),
            pltpu.VMEM((rows + 2 * rim, half), BF16),
            pltpu.VMEM((rows, c_dim), F32),
            pltpu.VMEM((rows, lanes), F32),
            pltpu.VMEM((rows, c_dim), F32),
            pltpu.VMEM((2, members, half, lanes), BF16),
            pltpu.VMEM((rows, lanes), BF16),
            pltpu.VMEM((rows, c_dim), F32),
            pltpu.VMEM((rows, c_dim), BF16),
            pltpu.VMEM((2, rim, c_dim), BF16),
            pltpu.VMEM((2, rim, c_dim), BF16),
            pltpu.VMEM((8, lanes), F32),
            pltpu.VMEM((n_xy, 1, lanes), F32),
            pltpu.VMEM((n_zc, 1, lanes), F32),
            dma((7,)),
            dma((2,)),
            dma((2,)),
            dma((2, 2 * XN)),
            dma((2, members)),
            dma((2,)),
            dma((2,)),
            dma((n_xy,)),
            dma((n_xy,)),
            dma((n_zc,)),
            dma((n_zc,)),
        ],
        compiler_params=pltpu.CompilerParams(
            collective_id=0, has_side_effects=True, vmem_limit_bytes=63 << 20
        ),
        name="crps_layer",
    )(
        latent_fields.reshape(rows, c_dim),
        neighbours,
        mix_weight,
        norm_gain.reshape(1, c_dim),
        output_projector,
        verifying_fields,
        area.reshape(1, rows),
    )
    return (out[None], loss.reshape(()))


def solution(mesh):
    in_specs = (P("ens", "grid", None), P(None, "grid"), P(), P(), P(), P(None, "grid"), P("grid"))
    out_specs = (P("ens", "grid", None), P())
    return jax.shard_map(shards, mesh=mesh, in_specs=in_specs, out_specs=out_specs, check_vma=False)
```

```python
import functools

import jax
import jax.numpy as jnp
from jax import lax
from jax.experimental import pallas as pl
from jax.experimental.pallas import tpu as pltpu
from jax.sharding import PartitionSpec as P

ZH, XN, ZL, YN, CORES = 2, 4, 8, 4, 2
MESH = pl.DeviceIdType.MESH
GAP = 0.01
F32, BF16 = jnp.float32, jnp.bfloat16


def dot(a, b, ca, cb):
    return lax.dot_general(a, b, (((ca,), (cb,)), ((), ())), preferred_element_type=F32)


def device(zh, x, zl, y, core):
    return (zh * XN + x, (zl * YN + y) * CORES + core)


def kernel(
    total_points,
    x_hbm,
    nb_hbm,
    w_hbm,
    gain_hbm,
    proj_hbm,
    ver_hbm,
    area_hbm,
    out_ref,
    loss_ref,
    ext,
    w,
    pin,
    pv,
    nb,
    gain,
    ver,
    area,
    vert,
    areat,
    at_i,
    at_e,
    unit,
    scale,
    slope,
    fld,
    fq,
    gq,
    gs,
    direct,
    gmb,
    gsend,
    garr,
    lacc,
    lone,
    ltwo,
    near_sem,
    far_sem,
    in_sem,
    halo_s,
    halo_r,
    fld_s,
    fld_r,
    g_s,
    g_r,
    gh_s,
    gh_r,
    l1_s,
    l1_r,
    l2_s,
    l2_r,
):
    rows, c_dim = x_hbm.shape
    rim = rows // 4
    half = rows // 2
    vars_n = proj_hbm.shape[0]
    lanes = pv.shape[0]
    members = ZH * XN
    part = half // XN
    e, g = lax.axis_index("ens"), lax.axis_index("grid")
    bands = lax.axis_size("grid")
    zh, x = e // XN, e % XN
    zl, y, core = g // (YN * CORES), (g // CORES) % YN, g % CORES
    has_left, has_right = g > 0, g < bands - 1
    left, right = (e, g - 1), (e, g + 1)

    def at_z(d, core_):
        z = (zh * ZL + zl + d + 2 * ZH * ZL) % (ZH * ZL)
        return device(z // ZL, x, z % ZL, y, core_)

    offsets = [d for d in range(-(ZL // 2) + 1, ZL // 2 + 1) if d]
    xy = [(dx, dy) for dx in range(XN) for dy in range(YN) if (dx, dy) != (0, 0)]
    to_xy = [device(zh, (x + dx) % XN, zl, (y + dy) % YN, core) for dx, dy in xy]
    zc = [(d, dc) for d in offsets for dc in range(CORES)]
    to_zc = [at_z(d, (core + dc) % CORES) for d, dc in zc]
    other_core = device(zh, x, zl, y, 1 - core)
    meet = [(dh, dx) for dx in range(XN) for dh in range(ZH) if (dh, dx) != (0, 0)]
    to_meet = [device((zh + dh) % ZH, (x + dx) % XN, zl, y, core) for dh, dx in meet]

    barrier = pltpu.get_barrier_semaphore()

    def hello(to):
        pl.semaphore_signal(barrier, inc=1, device_id=to, device_id_type=MESH)

    chip, chips = g // CORES, bands // CORES
    first, last = chip == 0, chip == chips - 1
    upper = core == 1
    far_hellos = (
        [device(zh, (x + dx) % XN, zl, (y + dy) % YN, 1) for dx, dy in xy]
        + [device(1 - zh, (x + dx) % XN, zl, y, 1) for dx in range(XN)]
        + [at_z(-d, 1) for d in offsets]
    )

    @pl.when(upper)
    def _():
        hello((e, g - 1))
        pl.when(jnp.logical_not(last))(lambda: hello((e, g + 1)))

    @pl.when(jnp.logical_and(jnp.logical_not(upper), jnp.logical_not(first)))
    def _():
        hello((e, g - CORES))

    for to in far_hellos:
        hello(to)

    loads = [
        pltpu.make_async_copy(nb_hbm, nb, in_sem.at[0]),
        pltpu.make_async_copy(x_hbm, ext.at[pl.ds(rim, rows)], in_sem.at[1]),
        pltpu.make_async_copy(gain_hbm, gain, in_sem.at[2]),
        pltpu.make_async_copy(w_hbm, w, in_sem.at[3]),
        pltpu.make_async_copy(proj_hbm, pin, in_sem.at[4]),
        pltpu.make_async_copy(ver_hbm, ver, in_sem.at[5]),
        pltpu.make_async_copy(area_hbm, area, in_sem.at[6]),
    ]
    for load in loads:
        load.start()

    @pl.when(jnp.logical_not(has_left))
    def _():
        ext[0:rim] = jnp.zeros((rim, c_dim), BF16)

    @pl.when(jnp.logical_not(has_right))
    def _():
        ext[rim + rows :] = jnp.zeros((rim, c_dim), BF16)

    def near_wait():
        @pl.when(jnp.logical_not(upper))
        def _():
            pl.semaphore_wait(barrier, 3 - first.astype(jnp.int32) - last.astype(jnp.int32))
            pl.semaphore_signal(near_sem, inc=1, device_id=other_core, device_id_type=MESH)

        @pl.when(upper)
        def _():
            pl.semaphore_wait(near_sem, 1)

    def far_wait():
        @pl.when(upper)
        def _():
            pl.semaphore_wait(barrier, CORES * len(far_hellos))
            pl.semaphore_signal(far_sem, inc=1, device_id=other_core, device_id_type=MESH)

        @pl.when(jnp.logical_not(upper))
        def _():
            pl.semaphore_wait(far_sem, 1)

    def remote(src, dst, s_sem, r_sem, to):
        return pltpu.make_async_remote_copy(
            src_ref=src, dst_ref=dst, send_sem=s_sem, recv_sem=r_sem, device_id=to, device_id_type=MESH
        )

    halo_left = remote(
        x_hbm.at[pl.ds(0, rim)], ext.at[pl.ds(rim + rows, rim)], halo_s.at[0], halo_r.at[1], left
    )
    halo_right = remote(
        x_hbm.at[pl.ds(rows - rim, rim)], ext.at[pl.ds(0, rim)], halo_s.at[1], halo_r.at[0], right
    )
    from_left = remote(ext.at[pl.ds(0, rim)], ext.at[pl.ds(0, rim)], halo_s.at[0], halo_r.at[0], left)
    from_right = remote(
        ext.at[pl.ds(rim + rows, rim)],
        ext.at[pl.ds(rim + rows, rim)],
        halo_s.at[1],
        halo_r.at[1],
        right,
    )

    loads[0].wait()
    near = pltpu.roll(nb[...] - (g * rows - rim), rows - rim, axis=1)

    def counts(first, size, lo):
        q = lax.broadcasted_iota(jnp.int32, (size, half), 0) + first
        total = jnp.zeros((size, half), F32)
        for k in range(nb.shape[0]):
            total = total + jnp.where(q == near[k : k + 1, lo : lo + half], 1.0, 0.0)
        return total.astype(BF16)

    at_i[...] = counts(rim, rows, 0)
    at_e[...] = counts(0, rows + 2 * rim, half)
    near_wait()
    pl.when(has_left)(halo_left.start)
    pl.when(has_right)(halo_right.start)

    def forward(c, state, at, window):
        mixed = state.astype(F32) + dot(at, window, 0, 0) * (1.0 / nb.shape[0])
        centre = mixed - jnp.mean(mixed, axis=-1, keepdims=True)
        r = lax.rsqrt(jnp.mean(centre * centre, axis=-1, keepdims=True) + 1e-05)
        xh = centre * r
        here = pl.ds(c * half, half)
        unit[here] = xh
        scale[here] = jnp.broadcast_to(r, (half, scale.shape[1]))
        normed = (xh * gain[...]).astype(BF16)
        pre = dot(normed, w[...], 1, 0)
        k0 = 0.7978845608028654
        sq = pre * pre
        t = jnp.tanh(k0 * pre * (1.0 + 0.044715 * sq))
        cdf = 0.5 * (1.0 + t)
        out = (state.astype(F32) + pre * cdf).astype(BF16)
        slope[here] = cdf + 0.5 * pre * (1.0 - t * t) * (k0 * (1.0 + 3 * 0.044715 * sq))
        fld[c] = dot(out, pv[...], 1, 1).astype(BF16)
        fq[c, e] = fld[c, pl.ds(pl.multiple_of(x * part, part), part)]

    loads[1].wait()
    loads[2].wait()
    loads[3].wait()
    loads[4].wait()
    pv[0 : vars_n // 16 * 16] = pin[0 : vars_n // 16 * 16]
    pv[vars_n // 16 * 16 :] = jnp.zeros((lanes - vars_n // 16 * 16, c_dim), BF16)
    pv[vars_n // 16 * 16 : vars_n] = pin[vars_n // 16 * 16 :]
    forward(0, ext[rim + rim : rim + rim + half], at_i[...], ext[rim : rim + rows])

    sent = []

    def field(c, i):
        (dh, dx), to = meet[i], to_meet[i]
        there = pl.ds(pl.multiple_of(((x + dx) % XN) * part, part), part)
        return remote(fld.at[c, there], fq.at[c, e], fld_s.at[c, i], fld_r.at[c, e], to)

    def send_fields(c):
        for i in range(len(meet)):
            field(c, i).start()

    @pl.when(zh > 0)
    def _():
        far_wait()
        send_fields(0)

    pl.when(has_left)(from_left.wait_recv)
    pl.when(has_right)(from_right.wait_recv)
    state_e = jnp.concatenate([ext[rows : rows + rim], ext[rim : 2 * rim]], axis=0)
    forward(1, state_e, at_e[...], ext[...])

    @pl.when(zh == 0)
    def _():
        far_wait()
        send_fields(0)

    send_fields(1)

    loads[5].wait()
    loads[6].wait()
    tall = jnp.concatenate([ver[...], jnp.zeros((lanes - vars_n, rows), F32)], axis=0)
    vert[...] = pltpu.roll(tall, rows - rim, axis=1).T
    areat[...] = pltpu.roll(jnp.broadcast_to(area[...], (lanes, rows)), rows - rim, axis=1).T
    lacc[...] = jnp.zeros(lacc.shape, F32)

    def score(c):
        for dh, dx in meet:
            m = ((zh + dh) % ZH) * XN + (x + dx) % XN
            remote(fq.at[c, m], fq.at[c, m], fld_s.at[c, 0], fld_r.at[c, m], other_core).wait_recv()
        pair = 1.0 / (members * (members - 1))
        step = 16
        for lo in range(0, part, step):
            f = [fq[c, m, lo : lo + step, :].astype(F32) for m in range(members)]
            there = pl.ds(pl.multiple_of(c * half + x * part + lo, step), step)
            truth, weight = vert[there], areat[there]
            good = jnp.zeros_like(truth)
            spread = jnp.zeros_like(truth)
            pull = []
            for m in range(members):
                d = f[m] - truth
                q = d * d + GAP
                root = lax.rsqrt(q)
                good = good + q * root
                pull.append((1.0 / members) * (d * root))
            for m in range(members):
                for n in range(m + 1, members):
                    d = f[m] - f[n]
                    q = d * d + GAP
                    root = lax.rsqrt(q)
                    spread = spread + q * root
                    slant = pair * (d * root)
                    pull[m] = pull[m] - slant
                    pull[n] = pull[n] + slant
            total = weight * (good * (1.0 / members) - pair * spread)
            lacc[...] += total[0:8] + total[8:16]
            for i in range(XN):
                mine = jnp.where(zh == 0, pull[i], pull[XN + i])
                gq[c, i, lo : lo + step, :] = (weight * mine).astype(BF16)

    def give(c, dx):
        to = device(zh, (x + dx) % XN, zl, y, core)
        here = gs.at[pl.ds(pl.multiple_of(c * half + x * part, part), part)]
        return remote(gq.at[c, (x + dx) % XN], here, g_s.at[c, dx], g_r.at[c, x], to)

    def send_g(c):
        for dx in range(1, XN):
            give(c, dx).start()
        gs[pl.ds(pl.multiple_of(c * half + x * part, part), part)] = gq[c, x]

    def wait_g(c):
        for dx in range(1, XN):
            i = (x + dx) % XN
            here = gs.at[pl.ds(pl.multiple_of(c * half + i * part, part), part)]
            remote(here, here, g_s.at[c, 0], g_r.at[c, i], other_core).wait_recv()

    def backward(c):
        here = pl.ds(c * half, half)
        grad_y = dot(gs[here], pv[...], 1, 0)
        grad_pre = (grad_y * slope[here]).astype(BF16)
        gx = dot(grad_pre, w[...], 1, 1) * gain[...]
        xh = unit[here]
        flat = jnp.mean(gx, axis=-1, keepdims=True)
        lean = jnp.mean(gx * xh, axis=-1, keepdims=True)
        gm = scale[here][:, 0:1] * (gx - flat - xh * lean)
        direct[here] = grad_y + gm
        gmb[here] = gm.astype(BF16)

    score(0)
    send_g(0)
    score(1)

    lane = lax.broadcasted_iota(jnp.int32, (1, lanes), 1)
    mine1 = x * YN + y
    lone[mine1] = jnp.where(lane < vars_n, jnp.sum(lacc[...], axis=0, keepdims=True), 0.0)
    for i, to in enumerate(to_xy):
        copy = remote(lone.at[mine1], lone.at[mine1], l1_s.at[i], l1_r.at[mine1], to)
        copy.start()
        sent.append(copy)

    send_g(1)
    wait_g(0)
    backward(0)
    wait_g(1)
    backward(1)
    per = 1.0 / nb.shape[0]
    gsend[0] = (dot(at_e[0:rim], gmb[half:], 1, 0) * per).astype(BF16)
    gsend[1] = (dot(at_e[rim + rows :], gmb[half:], 1, 0) * per).astype(BF16)
    grad_left = remote(gsend.at[0], garr.at[1], gh_s.at[0], gh_r.at[1], left)
    grad_right = remote(gsend.at[1], garr.at[0], gh_s.at[1], gh_r.at[0], right)
    pl.when(has_left)(grad_left.start)
    pl.when(has_right)(grad_right.start)

    for dx, dy in xy:
        slot = ((x + dx) % XN) * YN + (y + dy) % YN
        remote(lone.at[slot], lone.at[slot], l1_s.at[0], l1_r.at[slot], other_core).wait_recv()
    mine2 = zl * CORES + core
    acc = lone[0]
    for i in range(1, XN * YN):
        acc = acc + lone[i]
    ltwo[mine2] = acc
    for i, to in enumerate([other_core] + to_zc):
        copy = remote(ltwo.at[mine2], ltwo.at[mine2], l2_s.at[i], l2_r.at[mine2], to)
        copy.start()
        sent.append(copy)

    spread = (dot(at_i[...], gmb[0:half], 1, 0) + dot(at_e[rim : rim + rows], gmb[half:], 1, 0)) * per
    out_ref[rim : rim + half] = (spread[rim : rim + half] + direct[0:half]).astype(BF16)
    tail = spread[rows - rim :] + direct[half : half + rim]
    head = spread[0:rim] + direct[half + rim :]
    direct[half : half + rim] = tail
    direct[half + rim :] = head

    @pl.when(jnp.logical_not(has_left))
    def _():
        garr[0] = jnp.zeros((rim, c_dim), BF16)

    @pl.when(jnp.logical_not(has_right))
    def _():
        garr[1] = jnp.zeros((rim, c_dim), BF16)

    @pl.when(has_left)
    def _():
        remote(garr.at[0], garr.at[0], gh_s.at[0], gh_r.at[0], left).wait_recv()

    @pl.when(has_right)
    def _():
        remote(garr.at[1], garr.at[1], gh_s.at[1], gh_r.at[1], right).wait_recv()

    out_ref[0:rim] = (direct[half + rim :] + garr[0].astype(F32)).astype(BF16)
    out_ref[rows - rim :] = (direct[half : half + rim] + garr[1].astype(F32)).astype(BF16)

    for slot in range(ZL * CORES):

        @pl.when(slot != mine2)
        def _():
            remote(ltwo.at[slot], ltwo.at[slot], l2_s.at[0], l2_r.at[slot], other_core).wait_recv()

    acc = ltwo[0]
    for i in range(1, ZL * CORES):
        acc = acc + ltwo[i]
    loss = jnp.sum(acc, axis=-1, keepdims=True) * (1.0 / (total_points * vars_n))
    loss_ref[...] = jnp.broadcast_to(loss, loss_ref.shape)

    for copy in sent:
        copy.wait_send()
    for c in range(2):
        for i in range(len(meet)):
            field(c, i).wait_send()
        for dx in range(1, XN):
            give(c, dx).wait_send()
    pl.when(has_left)(halo_left.wait_send)
    pl.when(has_right)(halo_right.wait_send)
    pl.when(has_left)(grad_left.wait_send)
    pl.when(has_right)(grad_right.wait_send)


def store(made, total, out_hbm, loss_ref, sem):
    copy = pltpu.make_async_copy(made, out_hbm, sem)
    copy.start()
    loss_ref[...] = total[:, 0:1]
    copy.wait()


def shards(
    latent_fields, neighbours, mix_weight, norm_gain, output_projector, verifying_fields, area
):
    _, rows, c_dim = latent_fields.shape
    count = neighbours.shape[0]
    vars_n = output_projector.shape[0]
    rim, half, lanes = rows // 4, rows // 2, 128
    members = ZH * XN
    anywhere = pl.BlockSpec(memory_space=pl.ANY)
    dma = pltpu.SemaphoreType.DMA
    n_xy, n_zc = XN * YN, ZL * CORES
    out, loss = pl.pallas_call(
        functools.partial(kernel, rows * lax.axis_size("grid")),
        out_shape=(
            pltpu.VMEM((rows, c_dim), BF16),
            pltpu.VMEM((1, lanes), F32),
        ),
        in_specs=[anywhere] * 7,
        out_specs=(
            pl.BlockSpec(memory_space=pltpu.VMEM),
            pl.BlockSpec(memory_space=pltpu.VMEM),
        ),
        scratch_shapes=[
            pltpu.VMEM((rows + 2 * rim, c_dim), BF16),
            pltpu.VMEM(mix_weight.shape, BF16),
            pltpu.VMEM((vars_n, c_dim), BF16),
            pltpu.VMEM((lanes, c_dim), BF16),
            pltpu.VMEM((count, rows), jnp.int32),
            pltpu.VMEM((1, c_dim), F32),
            pltpu.VMEM((vars_n, rows), F32),
            pltpu.VMEM((1, rows), F32),
            pltpu.VMEM((rows, lanes), F32),
            pltpu.VMEM((rows, lanes), F32),
            pltpu.VMEM((rows, half), BF16),
            pltpu.VMEM((rows + 2 * rim, half), BF16),
            pltpu.VMEM((rows, c_dim), F32),
            pltpu.VMEM((rows, lanes), F32),
            pltpu.VMEM((rows, c_dim), F32),
            pltpu.VMEM((2, half, lanes), BF16),
            pltpu.VMEM((2, members, half // XN, lanes), BF16),
            pltpu.VMEM((2, XN, half // XN, lanes), BF16),
            pltpu.VMEM((rows, lanes), BF16),
            pltpu.VMEM((rows, c_dim), F32),
            pltpu.VMEM((rows, c_dim), BF16),
            pltpu.VMEM((2, rim, c_dim), BF16),
            pltpu.VMEM((2, rim, c_dim), BF16),
            pltpu.VMEM((8, lanes), F32),
            pltpu.VMEM((n_xy, 1, lanes), F32),
            pltpu.VMEM((n_zc, 1, lanes), F32),
            pltpu.SemaphoreType.REGULAR,
            pltpu.SemaphoreType.REGULAR,
            dma((7,)),
            dma((2,)),
            dma((2,)),
            dma((2, members)),
            dma((2, members)),
            dma((2, XN)),
            dma((2, XN)),
            dma((2,)),
            dma((2,)),
            dma((n_xy,)),
            dma((n_xy,)),
            dma((n_zc,)),
            dma((n_zc,)),
        ],
        compiler_params=pltpu.CompilerParams(
            collective_id=0, has_side_effects=True, vmem_limit_bytes=63 << 20
        ),
        name="crps_layer",
    )(
        latent_fields.reshape(rows, c_dim),
        neighbours,
        mix_weight,
        norm_gain.reshape(1, c_dim),
        output_projector,
        verifying_fields,
        area.reshape(1, rows),
    )
    out, loss = pl.pallas_call(
        store,
        out_shape=(
            jax.ShapeDtypeStruct((rows, c_dim), BF16),
            jax.ShapeDtypeStruct((1, 1), F32),
        ),
        in_specs=[pl.BlockSpec(memory_space=pltpu.VMEM)] * 2,
        out_specs=(anywhere, pl.BlockSpec(memory_space=pltpu.VMEM)),
        scratch_shapes=[dma(())],
        compiler_params=pltpu.CompilerParams(vmem_limit_bytes=16 << 20),
        name="store_result",
    )(out, loss)
    return (out[None], loss.reshape(()))


def solution(mesh):
    in_specs = (P("ens", "grid", None), P(None, "grid"), P(), P(), P(), P(None, "grid"), P("grid"))
    out_specs = (P("ens", "grid", None), P())
    return jax.shard_map(shards, mesh=mesh, in_specs=in_specs, out_specs=out_specs, check_vma=False)
```

```python
import functools

import jax
import jax.numpy as jnp
from jax import lax
from jax.experimental import pallas as pl
from jax.experimental.pallas import tpu as pltpu
from jax.sharding import PartitionSpec as P

ZH, XN, ZL, YN, CORES = 2, 4, 8, 4, 2
MESH = pl.DeviceIdType.MESH
GAP = 0.01
F32, BF16 = jnp.float32, jnp.bfloat16


def dot(a, b, ca, cb):
    return lax.dot_general(a, b, (((ca,), (cb,)), ((), ())), preferred_element_type=F32)


def device(zh, x, zl, y, core):
    return (zh * XN + x, (zl * YN + y) * CORES + core)


def kernel(
    total_points,
    x_hbm,
    nb_hbm,
    w_hbm,
    gain_hbm,
    proj_hbm,
    ver_hbm,
    area_hbm,
    out_ref,
    loss_ref,
    ext,
    w,
    pin,
    pv,
    nb,
    gain,
    ver,
    area,
    vert,
    areat,
    at_i,
    at_e,
    unit,
    scale,
    slope,
    fld,
    fq,
    gq,
    gs,
    direct,
    gmb,
    gsend,
    garr,
    lacc,
    lone,
    ltwo,
    near_sem,
    far_sem,
    in_sem,
    halo_s,
    halo_r,
    fld_s,
    fld_r,
    g_s,
    g_r,
    gh_s,
    gh_r,
    l1_s,
    l1_r,
    l2_s,
    l2_r,
):
    rows, c_dim = x_hbm.shape
    rim = rows // 4
    half = rows // 2
    vars_n = proj_hbm.shape[0]
    lanes = pv.shape[0]
    members = ZH * XN
    part = half // XN
    e, g = lax.axis_index("ens"), lax.axis_index("grid")
    bands = lax.axis_size("grid")
    zh, x = e // XN, e % XN
    zl, y, core = g // (YN * CORES), (g // CORES) % YN, g % CORES
    has_left, has_right = g > 0, g < bands - 1
    left, right = (e, g - 1), (e, g + 1)

    def at_z(d, core_):
        z = (zh * ZL + zl + d + 2 * ZH * ZL) % (ZH * ZL)
        return device(z // ZL, x, z % ZL, y, core_)

    offsets = [d for d in range(-(ZL // 2) + 1, ZL // 2 + 1) if d]
    xy = [(dx, dy) for dx in range(XN) for dy in range(YN) if (dx, dy) != (0, 0)]
    to_xy = [device(zh, (x + dx) % XN, zl, (y + dy) % YN, core) for dx, dy in xy]
    zc = [(d, dc) for d in offsets for dc in range(CORES)]
    to_zc = [at_z(d, (core + dc) % CORES) for d, dc in zc]
    other_core = device(zh, x, zl, y, 1 - core)
    meet = [(dh, dx) for dx in range(XN) for dh in range(ZH) if (dh, dx) != (0, 0)]
    to_meet = [device((zh + dh) % ZH, (x + dx) % XN, zl, y, core) for dh, dx in meet]

    barrier = pltpu.get_barrier_semaphore()

    def hello(to):
        pl.semaphore_signal(barrier, inc=1, device_id=to, device_id_type=MESH)

    chip, chips = g // CORES, bands // CORES
    first, last = chip == 0, chip == chips - 1
    upper = core == 1
    far_hellos = (
        [device(zh, (x + dx) % XN, zl, (y + dy) % YN, 1) for dx, dy in xy]
        + [device(1 - zh, (x + dx) % XN, zl, y, 1) for dx in range(XN)]
        + [at_z(-d, 1) for d in offsets]
    )

    @pl.when(upper)
    def _():
        hello((e, g - 1))
        pl.when(jnp.logical_not(last))(lambda: hello((e, g + 1)))

    @pl.when(jnp.logical_and(jnp.logical_not(upper), jnp.logical_not(first)))
    def _():
        hello((e, g - CORES))

    loads = [
        pltpu.make_async_copy(nb_hbm, nb, in_sem.at[0]),
        pltpu.make_async_copy(x_hbm, ext.at[pl.ds(rim, rows)], in_sem.at[1]),
        pltpu.make_async_copy(gain_hbm, gain, in_sem.at[2]),
        pltpu.make_async_copy(w_hbm, w, in_sem.at[3]),
        pltpu.make_async_copy(proj_hbm, pin, in_sem.at[4]),
        pltpu.make_async_copy(ver_hbm, ver, in_sem.at[5]),
        pltpu.make_async_copy(area_hbm, area, in_sem.at[6]),
    ]
    for load in loads:
        load.start()

    for to in far_hellos:
        hello(to)

    @pl.when(jnp.logical_not(has_left))
    def _():
        ext[0:rim] = jnp.zeros((rim, c_dim), BF16)

    @pl.when(jnp.logical_not(has_right))
    def _():
        ext[rim + rows :] = jnp.zeros((rim, c_dim), BF16)

    def near_wait():
        @pl.when(jnp.logical_not(upper))
        def _():
            pl.semaphore_wait(barrier, 3 - first.astype(jnp.int32) - last.astype(jnp.int32))
            pl.semaphore_signal(near_sem, inc=1, device_id=other_core, device_id_type=MESH)

        @pl.when(upper)
        def _():
            pl.semaphore_wait(near_sem, 1)

    def far_wait():
        @pl.when(upper)
        def _():
            pl.semaphore_wait(barrier, CORES * len(far_hellos))
            pl.semaphore_signal(far_sem, inc=1, device_id=other_core, device_id_type=MESH)

        @pl.when(jnp.logical_not(upper))
        def _():
            pl.semaphore_wait(far_sem, 1)

    def remote(src, dst, s_sem, r_sem, to):
        return pltpu.make_async_remote_copy(
            src_ref=src, dst_ref=dst, send_sem=s_sem, recv_sem=r_sem, device_id=to, device_id_type=MESH
        )

    halo_left = remote(
        x_hbm.at[pl.ds(0, rim)], ext.at[pl.ds(rim + rows, rim)], halo_s.at[0], halo_r.at[1], left
    )
    halo_right = remote(
        x_hbm.at[pl.ds(rows - rim, rim)], ext.at[pl.ds(0, rim)], halo_s.at[1], halo_r.at[0], right
    )
    from_left = remote(ext.at[pl.ds(0, rim)], ext.at[pl.ds(0, rim)], halo_s.at[0], halo_r.at[0], left)
    from_right = remote(
        ext.at[pl.ds(rim + rows, rim)],
        ext.at[pl.ds(rim + rows, rim)],
        halo_s.at[1],
        halo_r.at[1],
        right,
    )

    loads[0].wait()
    near = pltpu.roll(nb[...] - (g * rows - rim), rows - rim, axis=1)

    def counts(first, size, lo):
        q = lax.broadcasted_iota(jnp.int32, (size, half), 0) + first
        total = jnp.zeros((size, half), F32)
        for k in range(nb.shape[0]):
            total = total + jnp.where(q == near[k : k + 1, lo : lo + half], 1.0, 0.0)
        return total.astype(BF16)

    at_i[...] = counts(rim, rows, 0)
    at_e[...] = counts(0, rows + 2 * rim, half)
    near_wait()
    pl.when(has_left)(halo_left.start)
    pl.when(has_right)(halo_right.start)

    def forward(c, state, at, window):
        mixed = state.astype(F32) + dot(at, window, 0, 0) * (1.0 / nb.shape[0])
        centre = mixed - jnp.mean(mixed, axis=-1, keepdims=True)
        r = lax.rsqrt(jnp.mean(centre * centre, axis=-1, keepdims=True) + 1e-05)
        xh = centre * r
        here = pl.ds(c * half, half)
        unit[here] = xh
        scale[here] = jnp.broadcast_to(r, (half, scale.shape[1]))
        normed = (xh * gain[...]).astype(BF16)
        pre = dot(normed, w[...], 1, 0)
        k0 = 0.7978845608028654
        sq = pre * pre
        t = jnp.tanh(k0 * pre * (1.0 + 0.044715 * sq))
        cdf = 0.5 * (1.0 + t)
        out = (state.astype(F32) + pre * cdf).astype(BF16)
        slope[here] = cdf + 0.5 * pre * (1.0 - t * t) * (k0 * (1.0 + 3 * 0.044715 * sq))
        fld[c] = dot(out, pv[...], 1, 1).astype(BF16)
        fq[c, e] = fld[c, pl.ds(pl.multiple_of(x * part, part), part)]

    loads[1].wait()
    loads[2].wait()
    loads[3].wait()
    loads[4].wait()
    pv[0 : vars_n // 16 * 16] = pin[0 : vars_n // 16 * 16]
    pv[vars_n // 16 * 16 :] = jnp.zeros((lanes - vars_n // 16 * 16, c_dim), BF16)
    pv[vars_n // 16 * 16 : vars_n] = pin[vars_n // 16 * 16 :]
    forward(0, ext[rim + rim : rim + rim + half], at_i[...], ext[rim : rim + rows])

    def field(c, i):
        (dh, dx), to = meet[i], to_meet[i]
        there = pl.ds(pl.multiple_of(((x + dx) % XN) * part, part), part)
        return remote(fld.at[c, there], fq.at[c, e], fld_s.at[c], fld_r.at[c], to)

    def all_of(ref, count, s_sem, r_sem):
        some = ref.at[pl.ds(0, count)]
        return remote(some, some, s_sem, r_sem, other_core)

    def send_fields(c):
        for i in range(len(meet)):
            field(c, i).start()

    @pl.when(zh > 0)
    def _():
        far_wait()
        send_fields(0)

    pl.when(has_left)(from_left.wait_recv)
    pl.when(has_right)(from_right.wait_recv)
    state_e = jnp.concatenate([ext[rows : rows + rim], ext[rim : 2 * rim]], axis=0)
    forward(1, state_e, at_e[...], ext[...])

    @pl.when(zh == 0)
    def _():
        far_wait()
        send_fields(0)

    send_fields(1)

    loads[5].wait()
    loads[6].wait()
    tall = jnp.concatenate([ver[...], jnp.zeros((lanes - vars_n, rows), F32)], axis=0)
    vert[...] = pltpu.roll(tall, rows - rim, axis=1).T
    areat[...] = pltpu.roll(jnp.broadcast_to(area[...], (lanes, rows)), rows - rim, axis=1).T
    lacc[...] = jnp.zeros(lacc.shape, F32)

    def score(c):
        all_of(fq.at[c], len(meet), fld_s.at[c], fld_r.at[c]).wait_recv()
        pair = 1.0 / (members * (members - 1))
        step = 16
        for lo in range(0, part, step):
            f = [fq[c, m, lo : lo + step, :].astype(F32) for m in range(members)]
            there = pl.ds(pl.multiple_of(c * half + x * part + lo, step), step)
            truth, weight = vert[there], areat[there]
            good = jnp.zeros_like(truth)
            spread = jnp.zeros_like(truth)
            pull = []
            for m in range(members):
                d = f[m] - truth
                q = d * d + GAP
                root = lax.rsqrt(q)
                good = good + q * root
                pull.append((1.0 / members) * (d * root))
            for m in range(members):
                for n in range(m + 1, members):
                    d = f[m] - f[n]
                    q = d * d + GAP
                    root = lax.rsqrt(q)
                    spread = spread + q * root
                    slant = pair * (d * root)
                    pull[m] = pull[m] - slant
                    pull[n] = pull[n] + slant
            total = weight * (good * (1.0 / members) - pair * spread)
            lacc[...] += total[0:8] + total[8:16]
            for i in range(XN):
                mine = jnp.where(zh == 0, pull[i], pull[XN + i])
                gq[c, i, lo : lo + step, :] = (weight * mine).astype(BF16)

    def give(c, dx):
        to = device(zh, (x + dx) % XN, zl, y, core)
        here = gs.at[pl.ds(pl.multiple_of(c * half + x * part, part), part)]
        return remote(gq.at[c, (x + dx) % XN], here, g_s.at[c], g_r.at[c], to)

    def send_g(c):
        for dx in range(1, XN):
            give(c, dx).start()
        gs[pl.ds(pl.multiple_of(c * half + x * part, part), part)] = gq[c, x]

    def wait_g(c):
        all_of(gq.at[c], XN - 1, g_s.at[c], g_r.at[c]).wait_recv()

    def backward(c):
        here = pl.ds(c * half, half)
        grad_y = dot(gs[here], pv[...], 1, 0)
        grad_pre = (grad_y * slope[here]).astype(BF16)
        gx = dot(grad_pre, w[...], 1, 1) * gain[...]
        xh = unit[here]
        flat = jnp.mean(gx, axis=-1, keepdims=True)
        lean = jnp.mean(gx * xh, axis=-1, keepdims=True)
        gm = scale[here][:, 0:1] * (gx - flat - xh * lean)
        direct[here] = grad_y + gm
        gmb[here] = gm.astype(BF16)

    score(0)
    send_g(0)
    score(1)

    lane = lax.broadcasted_iota(jnp.int32, (1, lanes), 1)
    mine1 = x * YN + y
    lone[mine1] = jnp.where(lane < vars_n, jnp.sum(lacc[...], axis=0, keepdims=True), 0.0)
    for to in to_xy:
        copy = remote(lone.at[mine1], lone.at[mine1], l1_s, l1_r, to)
        copy.start()

    send_g(1)
    wait_g(0)
    backward(0)
    wait_g(1)
    backward(1)
    per = 1.0 / nb.shape[0]
    gsend[0] = (dot(at_e[0:rim], gmb[half:], 1, 0) * per).astype(BF16)
    gsend[1] = (dot(at_e[rim + rows :], gmb[half:], 1, 0) * per).astype(BF16)
    grad_left = remote(gsend.at[0], garr.at[1], gh_s.at[0], gh_r.at[1], left)
    grad_right = remote(gsend.at[1], garr.at[0], gh_s.at[1], gh_r.at[0], right)
    pl.when(has_left)(grad_left.start)
    pl.when(has_right)(grad_right.start)

    loss_one = all_of(lone, len(to_xy), l1_s, l1_r)
    loss_one.wait_recv()
    mine2 = zl * CORES + core
    acc = lone[0]
    for i in range(1, XN * YN):
        acc = acc + lone[i]
    ltwo[mine2] = acc
    for to in [other_core] + to_zc:
        copy = remote(ltwo.at[mine2], ltwo.at[mine2], l2_s, l2_r, to)
        copy.start()

    spread = (dot(at_i[...], gmb[0:half], 1, 0) + dot(at_e[rim : rim + rows], gmb[half:], 1, 0)) * per
    out_ref[rim : rim + half] = (spread[rim : rim + half] + direct[0:half]).astype(BF16)
    tail = spread[rows - rim :] + direct[half : half + rim]
    head = spread[0:rim] + direct[half + rim :]
    direct[half : half + rim] = tail
    direct[half + rim :] = head

    @pl.when(jnp.logical_not(has_left))
    def _():
        garr[0] = jnp.zeros((rim, c_dim), BF16)

    @pl.when(jnp.logical_not(has_right))
    def _():
        garr[1] = jnp.zeros((rim, c_dim), BF16)

    @pl.when(has_left)
    def _():
        remote(garr.at[0], garr.at[0], gh_s.at[0], gh_r.at[0], left).wait_recv()

    @pl.when(has_right)
    def _():
        remote(garr.at[1], garr.at[1], gh_s.at[1], gh_r.at[1], right).wait_recv()

    out_ref[0:rim] = (direct[half + rim :] + garr[0].astype(F32)).astype(BF16)
    out_ref[rows - rim :] = (direct[half : half + rim] + garr[1].astype(F32)).astype(BF16)

    loss_two = all_of(ltwo, 1 + len(to_zc), l2_s, l2_r)
    loss_two.wait_recv()
    acc = ltwo[0]
    for i in range(1, ZL * CORES):
        acc = acc + ltwo[i]
    loss = jnp.sum(acc, axis=-1, keepdims=True) * (1.0 / (total_points * vars_n))
    loss_ref[...] = jnp.broadcast_to(loss, loss_ref.shape)

    loss_one.wait_send()
    loss_two.wait_send()
    for c in range(2):
        all_of(fq.at[c], len(meet), fld_s.at[c], fld_r.at[c]).wait_send()
        all_of(gq.at[c], XN - 1, g_s.at[c], g_r.at[c]).wait_send()
    pl.when(has_left)(halo_left.wait_send)
    pl.when(has_right)(halo_right.wait_send)
    pl.when(has_left)(grad_left.wait_send)
    pl.when(has_right)(grad_right.wait_send)


def store(made, total, out_hbm, loss_ref, sem):
    copy = pltpu.make_async_copy(made, out_hbm, sem)
    copy.start()
    loss_ref[...] = total[:, 0:1]
    copy.wait()


def shards(
    latent_fields, neighbours, mix_weight, norm_gain, output_projector, verifying_fields, area
):
    _, rows, c_dim = latent_fields.shape
    count = neighbours.shape[0]
    vars_n = output_projector.shape[0]
    rim, half, lanes = rows // 4, rows // 2, 128
    members = ZH * XN
    anywhere = pl.BlockSpec(memory_space=pl.ANY)
    dma = pltpu.SemaphoreType.DMA
    n_xy, n_zc = XN * YN, ZL * CORES
    out, loss = pl.pallas_call(
        functools.partial(kernel, rows * lax.axis_size("grid")),
        out_shape=(
            pltpu.VMEM((rows, c_dim), BF16),
            pltpu.VMEM((1, lanes), F32),
        ),
        in_specs=[anywhere] * 7,
        out_specs=(
            pl.BlockSpec(memory_space=pltpu.VMEM),
            pl.BlockSpec(memory_space=pltpu.VMEM),
        ),
        scratch_shapes=[
            pltpu.VMEM((rows + 2 * rim, c_dim), BF16),
            pltpu.VMEM(mix_weight.shape, BF16),
            pltpu.VMEM((vars_n, c_dim), BF16),
            pltpu.VMEM((lanes, c_dim), BF16),
            pltpu.VMEM((count, rows), jnp.int32),
            pltpu.VMEM((1, c_dim), F32),
            pltpu.VMEM((vars_n, rows), F32),
            pltpu.VMEM((1, rows), F32),
            pltpu.VMEM((rows, lanes), F32),
            pltpu.VMEM((rows, lanes), F32),
            pltpu.VMEM((rows, half), BF16),
            pltpu.VMEM((rows + 2 * rim, half), BF16),
            pltpu.VMEM((rows, c_dim), F32),
            pltpu.VMEM((rows, lanes), F32),
            pltpu.VMEM((rows, c_dim), F32),
            pltpu.VMEM((2, half, lanes), BF16),
            pltpu.VMEM((2, members, half // XN, lanes), BF16),
            pltpu.VMEM((2, XN, half // XN, lanes), BF16),
            pltpu.VMEM((rows, lanes), BF16),
            pltpu.VMEM((rows, c_dim), F32),
            pltpu.VMEM((rows, c_dim), BF16),
            pltpu.VMEM((2, rim, c_dim), BF16),
            pltpu.VMEM((2, rim, c_dim), BF16),
            pltpu.VMEM((8, lanes), F32),
            pltpu.VMEM((n_xy, 1, lanes), F32),
            pltpu.VMEM((n_zc, 1, lanes), F32),
            pltpu.SemaphoreType.REGULAR,
            pltpu.SemaphoreType.REGULAR,
            dma((7,)),
            dma((2,)),
            dma((2,)),
            dma((2,)),
            dma((2,)),
            dma((2,)),
            dma((2,)),
            dma((2,)),
            dma((2,)),
            dma(()),
            dma(()),
            dma(()),
            dma(()),
        ],
        compiler_params=pltpu.CompilerParams(
            collective_id=0, has_side_effects=True, vmem_limit_bytes=63 << 20
        ),
        name="crps_layer",
    )(
        latent_fields.reshape(rows, c_dim),
        neighbours,
        mix_weight,
        norm_gain.reshape(1, c_dim),
        output_projector,
        verifying_fields,
        area.reshape(1, rows),
    )
    out, loss = pl.pallas_call(
        store,
        out_shape=(
            jax.ShapeDtypeStruct((rows, c_dim), BF16),
            jax.ShapeDtypeStruct((1, 1), F32),
        ),
        in_specs=[pl.BlockSpec(memory_space=pltpu.VMEM)] * 2,
        out_specs=(anywhere, pl.BlockSpec(memory_space=pltpu.VMEM)),
        scratch_shapes=[dma(())],
        compiler_params=pltpu.CompilerParams(vmem_limit_bytes=16 << 20),
        name="store_result",
    )(out, loss)
    return (out[None], loss.reshape(()))


def solution(mesh):
    in_specs = (P("ens", "grid", None), P(None, "grid"), P(), P(), P(), P(None, "grid"), P("grid"))
    out_specs = (P("ens", "grid", None), P())
    return jax.shard_map(shards, mesh=mesh, in_specs=in_specs, out_specs=out_specs, check_vma=False)
```

```python
import functools

import jax
import jax.numpy as jnp
from jax import lax
from jax.experimental import pallas as pl
from jax.experimental.pallas import tpu as pltpu
from jax.sharding import PartitionSpec as P

ZH, XN, ZL, YN, CORES = 2, 4, 8, 4, 2
MESH = pl.DeviceIdType.MESH
GAP = 0.01
F32, BF16 = jnp.float32, jnp.bfloat16


def dot(a, b, ca, cb):
    return lax.dot_general(a, b, (((ca,), (cb,)), ((), ())), preferred_element_type=F32)


def device(zh, x, zl, y, core):
    return (zh * XN + x, (zl * YN + y) * CORES + core)


def kernel(
    total_points,
    x_hbm,
    nb_hbm,
    w_hbm,
    gain_hbm,
    proj_hbm,
    ver_hbm,
    area_hbm,
    out_ref,
    loss_ref,
    ext,
    w,
    pin,
    pv,
    nb,
    gain,
    ver,
    area,
    vert,
    tall,
    at0,
    at1,
    unit,
    scale,
    slope,
    fld,
    fq0,
    fq1,
    gq0,
    gq1,
    gs,
    direct,
    gmb,
    tot,
    gsend,
    garr,
    lacc,
    lone,
    ltwo,
    near_sem,
    far_sem,
    in_sem,
    halo_s,
    halo_r,
    fq_s,
    fq_r,
    gq_s,
    gq_r,
    gh_s,
    gh_r,
    l1_s,
    l1_r,
    l2_s,
    l2_r,
):
    rows, c_dim = x_hbm.shape
    rim = rows // 4
    half = rows // 2
    vars_n = proj_hbm.shape[0]
    lanes = pv.shape[0]
    members = ZH * XN
    e, g = lax.axis_index("ens"), lax.axis_index("grid")
    bands = lax.axis_size("grid")
    zh, x = e // XN, e % XN
    zl, y, core = g // (YN * CORES), (g // CORES) % YN, g % CORES
    chip, chips = g // CORES, bands // CORES
    first, last = chip == 0, chip == chips - 1
    upper = core == 1
    has_far = jnp.where(upper, jnp.logical_not(last), jnp.logical_not(first))
    far = (e, g - 1 + 2 * core)

    base, size = (0, rows - rim), (rows - rim, rim)
    share = tuple(n // XN for n in size)
    fq, gq = (fq0, fq1), (gq0, gq1)

    def at_multiple(start, n):
        return pl.ds(pl.multiple_of(start, 16), n)

    near_rows = at_multiple((1 - core) * (rows - rim), rim)
    far_rows = at_multiple(core * (rows - rim), rim)
    near_halo = at_multiple((1 - core) * (rows + rim), rim)
    far_halo = at_multiple(core * (rows + rim), rim)

    def at_z(d, core_):
        z = (zh * ZL + zl + d + ZH * ZL) % (ZH * ZL)
        return device(z // ZL, x, z % ZL, y, core_)

    offsets = [d for d in range(-(ZL // 2) + 1, ZL // 2 + 1) if d]
    xy = [(dx, dy) for dx in range(XN) for dy in range(YN) if (dx, dy) != (0, 0)]
    to_xy = [device(zh, (x + dx) % XN, zl, (y + dy) % YN, core) for dx, dy in xy]
    zc = [(d, dc) for d in offsets for dc in range(CORES)]
    to_zc = [at_z(d, (core + dc) % CORES) for d, dc in zc]
    other_core = device(zh, x, zl, y, 1 - core)
    to_x = [device(zh, (x + dx) % XN, zl, y, core) for dx in range(1, XN)]
    meet = [(dh, dx) for dh in range(ZH - 1, -1, -1) for dx in range(XN) if (dh, dx) != (0, 0)]
    to_meet = [device((zh + dh) % ZH, (x + dx) % XN, zl, y, core) for dh, dx in meet]

    barrier = pltpu.get_barrier_semaphore()

    def hello(to):
        pl.semaphore_signal(barrier, inc=1, device_id=to, device_id_type=MESH)

    far_hellos = (
        [device(1 - zh, (x + dx) % XN, zl, y, 1) for dx in range(XN)]
        + [at_z(-d, 1) for d in offsets]
        + [device(zh, (x + dx) % XN, zl, (y + dy) % YN, 1) for dx, dy in xy]
    )

    @pl.when(upper)
    def _():
        hello((e, g - 1))
        pl.when(jnp.logical_not(last))(lambda: hello((e, g + 1)))

    @pl.when(jnp.logical_and(jnp.logical_not(upper), jnp.logical_not(first)))
    def _():
        hello((e, g - CORES))

    loads = [
        pltpu.make_async_copy(nb_hbm, nb, in_sem.at[0]),
        pltpu.make_async_copy(x_hbm, ext.at[pl.ds(rim, rows)], in_sem.at[1]),
        pltpu.make_async_copy(gain_hbm, gain, in_sem.at[2]),
        pltpu.make_async_copy(w_hbm, w, in_sem.at[3]),
        pltpu.make_async_copy(proj_hbm, pin, in_sem.at[4]),
        pltpu.make_async_copy(ver_hbm, ver, in_sem.at[5]),
        pltpu.make_async_copy(area_hbm, area, in_sem.at[6]),
    ]
    for load in loads:
        load.start()

    for to in far_hellos:
        hello(to)

    @pl.when(jnp.logical_not(has_far))
    def _():
        ext[far_halo] = jnp.zeros((rim, c_dim), BF16)

    def near_wait():
        @pl.when(jnp.logical_not(upper))
        def _():
            pl.semaphore_wait(barrier, 3 - first.astype(jnp.int32) - last.astype(jnp.int32))
            pl.semaphore_signal(near_sem, inc=1, device_id=other_core, device_id_type=MESH)

        @pl.when(upper)
        def _():
            pl.semaphore_wait(near_sem, 1)

    def far_wait():
        @pl.when(upper)
        def _():
            pl.semaphore_wait(barrier, CORES * len(far_hellos))
            pl.semaphore_signal(far_sem, inc=1, device_id=other_core, device_id_type=MESH)

        @pl.when(jnp.logical_not(upper))
        def _():
            pl.semaphore_wait(far_sem, 1)

    def remote(src, dst, s_sem, r_sem, to):
        return pltpu.make_async_remote_copy(
            src_ref=src, dst_ref=dst, send_sem=s_sem, recv_sem=r_sem, device_id=to, device_id_type=MESH
        )

    halo_near = remote(
        x_hbm.at[near_rows],
        ext.at[at_multiple(core * (rows + rim), rim)],
        halo_s.at[0],
        halo_r.at[0],
        other_core,
    )
    halo_far = remote(
        x_hbm.at[far_rows],
        ext.at[at_multiple((1 - core) * (rows + rim), rim)],
        halo_s.at[1],
        halo_r.at[1],
        far,
    )
    from_near = remote(ext.at[near_halo], ext.at[near_halo], halo_s.at[0], halo_r.at[0], other_core)
    from_far = remote(ext.at[far_halo], ext.at[far_halo], halo_s.at[1], halo_r.at[1], far)

    loads[0].wait()
    near = pltpu.roll(nb[...] - (g * rows - rim), rows - rim, axis=1)
    ends = near[:, half:]
    near = jnp.concatenate([near[:, :half], jnp.where(upper, pltpu.roll(ends, rim, axis=1), ends)], axis=1)
    start0 = (1 - core) * rim
    start1 = core * (rows - rim)

    def counts(start, height, lo, width):
        q = lax.broadcasted_iota(jnp.int32, (height, width), 0) + start
        total = jnp.zeros((height, width), F32)
        for k in range(nb.shape[0]):
            total = total + jnp.where(q == near[k : k + 1, lo : lo + width], 1.0, 0.0)
        return total.astype(BF16)

    at0[...] = counts(start0, rows + rim, 0, size[0])
    at1[...] = counts(start1, rows - rim, base[1], size[1])
    near_wait()
    halo_near.start()
    pl.when(has_far)(halo_far.start)

    def forward(c, state, at, window):
        mixed = state.astype(F32) + dot(at, window, 0, 0) * (1.0 / nb.shape[0])
        centre = mixed - jnp.mean(mixed, axis=-1, keepdims=True)
        r = lax.rsqrt(jnp.mean(centre * centre, axis=-1, keepdims=True) + 1e-05)
        xh = centre * r
        here = pl.ds(base[c], size[c])
        unit[here] = xh
        scale[here] = jnp.broadcast_to(r, (size[c], scale.shape[1]))
        normed = (xh * gain[...]).astype(BF16)
        pre = dot(normed, w[...], 1, 0)
        k0 = 0.7978845608028654
        sq = pre * pre
        t = jnp.tanh(k0 * pre * (1.0 + 0.044715 * sq))
        cdf = 0.5 * (1.0 + t)
        out = (state.astype(F32) + pre * cdf).astype(BF16)
        slope[here] = cdf + 0.5 * pre * (1.0 - t * t) * (k0 * (1.0 + 3 * 0.044715 * sq))
        fld[here] = dot(out, pv[...], 1, 1).astype(BF16)
        fq[c][e] = fld[at_multiple(base[c] + x * share[c], share[c])]

    loads[1].wait()
    loads[2].wait()
    loads[3].wait()
    loads[4].wait()
    pv[0 : vars_n // 16 * 16] = pin[0 : vars_n // 16 * 16]
    pv[vars_n // 16 * 16 :] = jnp.zeros((lanes - vars_n // 16 * 16, c_dim), BF16)
    pv[vars_n // 16 * 16 : vars_n] = pin[vars_n // 16 * 16 :]
    from_near.wait_recv()
    quarter = ext[at_multiple(rim + (1 - core) * (rows - rim), rim)]
    state = jnp.concatenate([ext[2 * rim : 2 * rim + half], quarter], axis=0)
    forward(0, state, at0[...], ext[at_multiple(start0, rows + rim)])

    loads[5].wait()
    loads[6].wait()
    vert[0:vars_n] = ver[...]
    vert[vars_n:] = jnp.broadcast_to(area[...], (lanes - vars_n, rows))
    turned = pltpu.roll(vert[...], rows - rim, axis=1).T
    tall[0:half] = turned[0:half]
    tall[at_multiple(half + core * rim, rim)] = turned[half : half + rim]
    tall[at_multiple(half + (1 - core) * rim, rim)] = turned[half + rim :]
    lacc[...] = jnp.zeros(lacc.shape, F32)

    def shared(c, i):
        (dh, dx), to = meet[i], to_meet[i]
        there = at_multiple(base[c] + ((x + dx) % XN) * share[c], share[c])
        return remote(fld.at[there], fq[c].at[e], fq_s.at[c], fq_r.at[c], to)

    def send_fields(c):
        for i in range(len(meet)):
            shared(c, i).start()

    def all_of(ref, count, s_sem, r_sem):
        some = ref.at[pl.ds(0, count)]
        return remote(some, some, s_sem, r_sem, other_core)

    @pl.when(zh > 0)
    def _():
        far_wait()
        send_fields(0)

    pl.when(has_far)(from_far.wait_recv)
    quarter = ext[at_multiple(rim + core * (rows - rim), rim)]
    forward(1, quarter, at1[...], ext[at_multiple(start1, rows - rim)])

    @pl.when(zh == 0)
    def _():
        far_wait()
        send_fields(0)

    send_fields(1)

    lane = lax.broadcasted_iota(jnp.int32, (1, lanes), 1)
    pair = 1.0 / (members * (members - 1))

    def score(c):
        all_of(fq[c], len(meet), fq_s.at[c], fq_r.at[c]).wait_recv()
        step = 16
        for lo in range(0, share[c], step):
            f = [fq[c][m, lo : lo + step, :].astype(F32) for m in range(members)]
            want = tall[at_multiple(base[c] + x * share[c] + lo, step)]
            weight = want[:, lanes - 1 :]
            want = jnp.where(lane < vars_n, want, 0.0)
            good = jnp.zeros_like(want)
            spread = jnp.zeros_like(want)
            pull = []
            for m in range(members):
                d = f[m] - want
                q = d * d + GAP
                root = lax.rsqrt(q)
                good = good + q * root
                pull.append((1.0 / members) * (d * root))
            for m in range(members):
                for n in range(m + 1, members):
                    d = f[m] - f[n]
                    q = d * d + GAP
                    root = lax.rsqrt(q)
                    spread = spread + q * root
                    slant = pair * (d * root)
                    pull[m] = pull[m] - slant
                    pull[n] = pull[n] + slant
            total = weight * (good * (1.0 / members) - pair * spread)
            lacc[...] += total[0:8] + total[8:16]
            for i in range(XN):
                mine = jnp.where(zh == 0, pull[i], pull[XN + i])
                gq[c][i, lo : lo + step, :] = (weight * mine).astype(BF16)

    def send_g(c):
        here = at_multiple(base[c] + x * share[c], share[c])
        for dx in range(1, XN):
            src = gq[c].at[(x + dx) % XN]
            remote(src, gs.at[here], gq_s.at[c], gq_r.at[c], to_x[dx - 1]).start()
        gs[here] = gq[c][x]

    def wait_g(c):
        all_of(gq[c], XN - 1, gq_s.at[c], gq_r.at[c]).wait_recv()

    def backward(c):
        here = pl.ds(base[c], size[c])
        grad_y = dot(gs[here], pv[...], 1, 0)
        grad_pre = (grad_y * slope[here]).astype(BF16)
        gx = dot(grad_pre, w[...], 1, 1) * gain[...]
        xh = unit[here]
        flat = jnp.mean(gx, axis=-1, keepdims=True)
        lean = jnp.mean(gx * xh, axis=-1, keepdims=True)
        gm = scale[here][:, 0:1] * (gx - flat - xh * lean)
        direct[here] = grad_y + gm
        gmb[here] = gm.astype(BF16)

    score(0)
    send_g(0)
    score(1)
    mine1 = x * YN + y
    lone[mine1] = jnp.where(lane < vars_n, jnp.sum(lacc[...], axis=0, keepdims=True), 0.0)
    for to in to_xy:
        remote(lone.at[mine1], lone.at[mine1], l1_s, l1_r, to).start()
    send_g(1)
    per = 1.0 / nb.shape[0]

    wait_g(1)
    backward(1)
    block = gmb[base[1] :]
    gsend[1] = (dot(at1[at_multiple(core * half, rim), :], block, 1, 0) * per).astype(BF16)
    grad_far = remote(gsend.at[1], garr.at[1], gh_s.at[1], gh_r.at[1], far)
    pl.when(has_far)(grad_far.start)

    wait_g(0)
    backward(0)
    wide = gmb[0 : size[0]]
    gsend[0] = (dot(at0[at_multiple((1 - core) * rows, rim), :], wide, 1, 0) * per).astype(BF16)
    grad_near = remote(gsend.at[0], garr.at[0], gh_s.at[0], gh_r.at[0], other_core)
    grad_near.start()

    loss_one = all_of(lone, len(to_xy), l1_s, l1_r)
    loss_one.wait_recv()
    mine2 = zl * CORES + core
    acc = lone[0]
    for i in range(1, XN * YN):
        acc = acc + lone[i]
    ltwo[mine2] = acc
    for to in [other_core] + to_zc:
        remote(ltwo.at[mine2], ltwo.at[mine2], l2_s, l2_r, to).start()

    tot[...] = dot(at0[at_multiple(core * rim, rows), :], wide, 1, 0) * per
    tot[rim : rim + half] += direct[0:half]
    tot[near_rows] += direct[half : half + rim]
    tot[at_multiple(core * half, half)] += dot(at1[at_multiple((1 - core) * rim, half), :], block, 1, 0) * per
    tot[far_rows] += direct[base[1] :]
    remote(garr.at[0], garr.at[0], gh_s.at[0], gh_r.at[0], other_core).wait_recv()
    tot[near_rows] += garr[0].astype(F32)
    out_ref[...] = tot[...].astype(BF16)

    @pl.when(has_far)
    def _():
        remote(garr.at[1], garr.at[1], gh_s.at[1], gh_r.at[1], far).wait_recv()
        out_ref[far_rows] = (tot[far_rows] + garr[1].astype(F32)).astype(BF16)

    loss_two = all_of(ltwo, 1 + len(to_zc), l2_s, l2_r)
    loss_two.wait_recv()
    acc = ltwo[0]
    for i in range(1, ZL * CORES):
        acc = acc + ltwo[i]
    loss = jnp.sum(acc, axis=-1, keepdims=True) * (1.0 / (total_points * vars_n))
    loss_ref[...] = jnp.broadcast_to(loss, loss_ref.shape)

    loss_one.wait_send()
    loss_two.wait_send()
    for c in range(2):
        all_of(fq[c], len(meet), fq_s.at[c], fq_r.at[c]).wait_send()
        all_of(gq[c], XN - 1, gq_s.at[c], gq_r.at[c]).wait_send()
    halo_near.wait_send()
    grad_near.wait_send()
    pl.when(has_far)(halo_far.wait_send)
    pl.when(has_far)(grad_far.wait_send)


def store(made, total, out_hbm, loss_hbm, one, sem):
    copy = pltpu.make_async_copy(made, out_hbm, sem.at[0])
    copy.start()
    one[...] = total[:, 0:1]
    small = pltpu.make_async_copy(one, loss_hbm, sem.at[1])
    small.start()
    copy.wait()
    small.wait()


def shards(
    latent_fields, neighbours, mix_weight, norm_gain, output_projector, verifying_fields, area
):
    _, rows, c_dim = latent_fields.shape
    count = neighbours.shape[0]
    vars_n = output_projector.shape[0]
    rim, lanes = rows // 4, 128
    members = ZH * XN
    anywhere = pl.BlockSpec(memory_space=pl.ANY)
    dma = pltpu.SemaphoreType.DMA
    n_xy, n_zc = XN * YN, ZL * CORES
    out, loss = pl.pallas_call(
        functools.partial(kernel, rows * lax.axis_size("grid")),
        out_shape=(
            pltpu.VMEM((rows, c_dim), BF16),
            pltpu.VMEM((1, lanes), F32),
        ),
        in_specs=[anywhere] * 7,
        out_specs=(
            pl.BlockSpec(memory_space=pltpu.VMEM),
            pl.BlockSpec(memory_space=pltpu.VMEM),
        ),
        scratch_shapes=[
            pltpu.VMEM((rows + 2 * rim, c_dim), BF16),
            pltpu.VMEM(mix_weight.shape, BF16),
            pltpu.VMEM((vars_n, c_dim), BF16),
            pltpu.VMEM((lanes, c_dim), BF16),
            pltpu.VMEM((count, rows), jnp.int32),
            pltpu.VMEM((1, c_dim), F32),
            pltpu.VMEM((vars_n, rows), F32),
            pltpu.VMEM((1, rows), F32),
            pltpu.VMEM((lanes, rows), F32),
            pltpu.VMEM((rows, lanes), F32),
            pltpu.VMEM((rows + rim, rows - rim), BF16),
            pltpu.VMEM((rows - rim, rim), BF16),
            pltpu.VMEM((rows, c_dim), F32),
            pltpu.VMEM((rows, lanes), F32),
            pltpu.VMEM((rows, c_dim), F32),
            pltpu.VMEM((rows, lanes), BF16),
            pltpu.VMEM((members, (rows - rim) // XN, lanes), BF16),
            pltpu.VMEM((members, rim // XN, lanes), BF16),
            pltpu.VMEM((XN, (rows - rim) // XN, lanes), BF16),
            pltpu.VMEM((XN, rim // XN, lanes), BF16),
            pltpu.VMEM((rows, lanes), BF16),
            pltpu.VMEM((rows, c_dim), F32),
            pltpu.VMEM((rows, c_dim), BF16),
            pltpu.VMEM((rows, c_dim), F32),
            pltpu.VMEM((2, rim, c_dim), BF16),
            pltpu.VMEM((2, rim, c_dim), BF16),
            pltpu.VMEM((8, lanes), F32),
            pltpu.VMEM((n_xy, 1, lanes), F32),
            pltpu.VMEM((n_zc, 1, lanes), F32),
            pltpu.SemaphoreType.REGULAR,
            pltpu.SemaphoreType.REGULAR,
            dma((7,)),
            dma((2,)),
            dma((2,)),
            dma((2,)),
            dma((2,)),
            dma((2,)),
            dma((2,)),
            dma((2,)),
            dma((2,)),
            dma(()),
            dma(()),
            dma(()),
            dma(()),
        ],
        compiler_params=pltpu.CompilerParams(
            collective_id=0, has_side_effects=True, vmem_limit_bytes=63 << 20
        ),
        name="crps_layer",
    )(
        latent_fields.reshape(rows, c_dim),
        neighbours,
        mix_weight,
        norm_gain.reshape(1, c_dim),
        output_projector,
        verifying_fields,
        area.reshape(1, rows),
    )
    out, loss = pl.pallas_call(
        store,
        out_shape=(
            jax.ShapeDtypeStruct((rows, c_dim), BF16),
            jax.ShapeDtypeStruct((1, 1), F32),
        ),
        in_specs=[pl.BlockSpec(memory_space=pltpu.VMEM)] * 2,
        out_specs=(anywhere, anywhere),
        scratch_shapes=[pltpu.VMEM((1, 1), F32), dma((2,))],
        compiler_params=pltpu.CompilerParams(vmem_limit_bytes=16 << 20),
        name="store_result",
    )(out, loss)
    return (out[None], loss.reshape(()))


def solution(mesh):
    in_specs = (P("ens", "grid", None), P(None, "grid"), P(), P(), P(), P(None, "grid"), P("grid"))
    out_specs = (P("ens", "grid", None), P())
    return jax.shard_map(shards, mesh=mesh, in_specs=in_specs, out_specs=out_specs, check_vma=False)
```

```python
import functools

import jax
import jax.numpy as jnp
from jax import lax
from jax.experimental import pallas as pl
from jax.experimental.pallas import tpu as pltpu
from jax.sharding import PartitionSpec as P

ZH, XN, ZL, YN, CORES = 2, 4, 8, 4, 2
MESH = pl.DeviceIdType.MESH
GAP = 0.01
F32, BF16 = jnp.float32, jnp.bfloat16


def dot(a, b, ca, cb):
    return lax.dot_general(a, b, (((ca,), (cb,)), ((), ())), preferred_element_type=F32)


def device(zh, x, zl, y, core):
    return (zh * XN + x, (zl * YN + y) * CORES + core)


def kernel(
    total_points,
    x_hbm,
    nb_hbm,
    w_hbm,
    gain_hbm,
    proj_hbm,
    ver_hbm,
    area_hbm,
    out_ref,
    loss_ref,
    ext,
    w,
    pin,
    pv,
    nb,
    gain,
    ver,
    area,
    vert,
    tall,
    at0,
    at1,
    unit,
    scale,
    slope,
    fld,
    fq0,
    fq1,
    gq0,
    gq1,
    gs,
    direct,
    gmb,
    tot,
    gsend,
    garr,
    lacc,
    lone,
    ltwo,
    near_sem,
    far_sem,
    in_sem,
    halo_s,
    halo_r,
    fq_s,
    fq_r,
    gq_s,
    gq_r,
    gh_s,
    gh_r,
    l1_s,
    l1_r,
    l2_s,
    l2_r,
):
    rows, c_dim = x_hbm.shape
    rim = rows // 4
    half = rows // 2
    vars_n = proj_hbm.shape[0]
    lanes = pv.shape[0]
    members = ZH * XN
    e, g = lax.axis_index("ens"), lax.axis_index("grid")
    bands = lax.axis_size("grid")
    zh, x = e // XN, e % XN
    zl, y, core = g // (YN * CORES), (g // CORES) % YN, g % CORES
    chip, chips = g // CORES, bands // CORES
    first, last = chip == 0, chip == chips - 1
    upper = core == 1
    has_far = jnp.where(upper, jnp.logical_not(last), jnp.logical_not(first))
    far = (e, g - 1 + 2 * core)

    base, size = (0, rows - rim), (rows - rim, rim)
    share = tuple(n // XN for n in size)
    fq, gq = (fq0, fq1), (gq0, gq1)

    def at_multiple(start, n):
        return pl.ds(pl.multiple_of(start, 16), n)

    near_rows = at_multiple((1 - core) * (rows - rim), rim)
    far_rows = at_multiple(core * (rows - rim), rim)
    near_halo = at_multiple((1 - core) * (rows + rim), rim)
    far_halo = at_multiple(core * (rows + rim), rim)

    def at_z(d, core_):
        z = (zh * ZL + zl + d + ZH * ZL) % (ZH * ZL)
        return device(z // ZL, x, z % ZL, y, core_)

    offsets = [d for d in range(-(ZL // 2) + 1, ZL // 2 + 1) if d]
    xy = [(dx, dy) for dx in range(XN) for dy in range(YN) if (dx, dy) != (0, 0)]
    to_xy = [device(zh, (x + dx) % XN, zl, (y + dy) % YN, core) for dx, dy in xy]
    zc = [(d, dc) for d in offsets for dc in range(CORES)]
    to_zc = [at_z(d, (core + dc) % CORES) for d, dc in zc]
    other_core = device(zh, x, zl, y, 1 - core)
    to_x = [device(zh, (x + dx) % XN, zl, y, core) for dx in range(1, XN)]
    meet = [(dh, dx) for dh in range(ZH - 1, -1, -1) for dx in range(XN) if (dh, dx) != (0, 0)]
    to_meet = [device((zh + dh) % ZH, (x + dx) % XN, zl, y, core) for dh, dx in meet]

    barrier = pltpu.get_barrier_semaphore()

    def hello(to):
        pl.semaphore_signal(barrier, inc=1, device_id=to, device_id_type=MESH)

    far_hellos = (
        [device(1 - zh, (x + dx) % XN, zl, y, 1) for dx in range(XN)]
        + [at_z(-d, 1) for d in offsets]
        + [device(zh, (x + dx) % XN, zl, (y + dy) % YN, 1) for dx, dy in xy]
    )

    @pl.when(upper)
    def _():
        hello((e, g - 1))
        pl.when(jnp.logical_not(last))(lambda: hello((e, g + 1)))

    @pl.when(jnp.logical_and(jnp.logical_not(upper), jnp.logical_not(first)))
    def _():
        hello((e, g - CORES))

    loads = [
        pltpu.make_async_copy(nb_hbm, nb, in_sem.at[0]),
        pltpu.make_async_copy(x_hbm, ext.at[pl.ds(rim, rows)], in_sem.at[1]),
        pltpu.make_async_copy(gain_hbm, gain, in_sem.at[2]),
        pltpu.make_async_copy(w_hbm, w, in_sem.at[3]),
        pltpu.make_async_copy(proj_hbm, pin, in_sem.at[4]),
        pltpu.make_async_copy(ver_hbm, ver, in_sem.at[5]),
        pltpu.make_async_copy(area_hbm, area, in_sem.at[6]),
    ]
    for load in loads:
        load.start()

    for to in far_hellos:
        hello(to)

    @pl.when(jnp.logical_not(has_far))
    def _():
        ext[far_halo] = jnp.zeros((rim, c_dim), BF16)

    def near_wait():
        @pl.when(jnp.logical_not(upper))
        def _():
            pl.semaphore_wait(barrier, 3 - first.astype(jnp.int32) - last.astype(jnp.int32))
            pl.semaphore_signal(near_sem, inc=1, device_id=other_core, device_id_type=MESH)

        @pl.when(upper)
        def _():
            pl.semaphore_wait(near_sem, 1)

    def far_wait():
        @pl.when(upper)
        def _():
            pl.semaphore_wait(barrier, CORES * len(far_hellos))
            pl.semaphore_signal(far_sem, inc=1, device_id=other_core, device_id_type=MESH)

        @pl.when(jnp.logical_not(upper))
        def _():
            pl.semaphore_wait(far_sem, 1)

    def remote(src, dst, s_sem, r_sem, to):
        return pltpu.make_async_remote_copy(
            src_ref=src, dst_ref=dst, send_sem=s_sem, recv_sem=r_sem, device_id=to, device_id_type=MESH
        )

    halo_near = remote(
        x_hbm.at[near_rows],
        ext.at[at_multiple(core * (rows + rim), rim)],
        halo_s.at[0],
        halo_r.at[0],
        other_core,
    )
    halo_far = remote(
        x_hbm.at[far_rows],
        ext.at[at_multiple((1 - core) * (rows + rim), rim)],
        halo_s.at[1],
        halo_r.at[1],
        far,
    )
    from_near = remote(ext.at[near_halo], ext.at[near_halo], halo_s.at[0], halo_r.at[0], other_core)
    from_far = remote(ext.at[far_halo], ext.at[far_halo], halo_s.at[1], halo_r.at[1], far)

    loads[0].wait()
    near = pltpu.roll(nb[...] - (g * rows - rim), rows - rim, axis=1)
    ends = near[:, half:]
    near = jnp.concatenate([near[:, :half], jnp.where(upper, pltpu.roll(ends, rim, axis=1), ends)], axis=1)
    start0 = (1 - core) * rim
    start1 = core * (rows - rim)

    def counts(start, height, lo, width):
        q = lax.broadcasted_iota(jnp.int32, (height, width), 0) + start
        total = jnp.zeros((height, width), F32)
        for k in range(nb.shape[0]):
            total = total + jnp.where(q == near[k : k + 1, lo : lo + width], 1.0, 0.0)
        return total.astype(BF16)

    at0[...] = counts(start0, rows + rim, 0, size[0])
    at1[...] = counts(start1, rows - rim, base[1], size[1])
    near_wait()
    halo_near.start()
    pl.when(has_far)(halo_far.start)

    def coded(f):
        most = jnp.max(jnp.abs(f), axis=-1, keepdims=True)
        power = jnp.ceil(jnp.log2(jnp.maximum(most, 1e-30)))
        code = jnp.where(lane < lanes - 1, jnp.round(f * jnp.exp2(14.0 - power)), power)
        return code.astype(jnp.int32).astype(jnp.int16)

    def decoded(code):
        f = code.astype(jnp.int32).astype(F32)
        return jnp.where(lane < vars_n, f * jnp.exp2(f[:, lanes - 1 :] - 14.0), 0.0)

    lane = lax.broadcasted_iota(jnp.int32, (1, lanes), 1)

    def forward(c, state, at, window):
        mixed = state.astype(F32) + dot(at, window, 0, 0) * (1.0 / nb.shape[0])
        centre = mixed - jnp.mean(mixed, axis=-1, keepdims=True)
        r = lax.rsqrt(jnp.mean(centre * centre, axis=-1, keepdims=True) + 1e-05)
        xh = centre * r
        here = pl.ds(base[c], size[c])
        unit[here] = xh
        scale[here] = jnp.broadcast_to(r, (size[c], scale.shape[1]))
        normed = (xh * gain[...]).astype(BF16)
        pre = dot(normed, w[...], 1, 0)
        k0 = 0.7978845608028654
        sq = pre * pre
        t = jnp.tanh(k0 * pre * (1.0 + 0.044715 * sq))
        cdf = 0.5 * (1.0 + t)
        out = (state.astype(F32) + pre * cdf).astype(BF16)
        slope[here] = cdf + 0.5 * pre * (1.0 - t * t) * (k0 * (1.0 + 3 * 0.044715 * sq))
        fld[here] = coded(dot(out, pv[...], 1, 1))
        fq[c][e] = fld[at_multiple(base[c] + x * share[c], share[c])]

    loads[1].wait()
    loads[2].wait()
    loads[3].wait()
    loads[4].wait()
    pv[0 : vars_n // 16 * 16] = pin[0 : vars_n // 16 * 16]
    pv[vars_n // 16 * 16 :] = jnp.zeros((lanes - vars_n // 16 * 16, c_dim), BF16)
    pv[vars_n // 16 * 16 : vars_n] = pin[vars_n // 16 * 16 :]
    from_near.wait_recv()
    quarter = ext[at_multiple(rim + (1 - core) * (rows - rim), rim)]
    state = jnp.concatenate([ext[2 * rim : 2 * rim + half], quarter], axis=0)
    forward(0, state, at0[...], ext[at_multiple(start0, rows + rim)])

    loads[5].wait()
    loads[6].wait()
    vert[0:vars_n] = ver[...]
    vert[vars_n:] = jnp.broadcast_to(area[...], (lanes - vars_n, rows))
    turned = pltpu.roll(vert[...], rows - rim, axis=1).T
    tall[0:half] = turned[0:half]
    tall[at_multiple(half + core * rim, rim)] = turned[half : half + rim]
    tall[at_multiple(half + (1 - core) * rim, rim)] = turned[half + rim :]
    lacc[...] = jnp.zeros(lacc.shape, F32)

    def shared(c, i):
        (dh, dx), to = meet[i], to_meet[i]
        there = at_multiple(base[c] + ((x + dx) % XN) * share[c], share[c])
        return remote(fld.at[there], fq[c].at[e], fq_s.at[c], fq_r.at[c], to)

    def send_fields(c):
        for i in range(len(meet)):
            shared(c, i).start()

    def all_of(ref, count, s_sem, r_sem):
        some = ref.at[pl.ds(0, count)]
        return remote(some, some, s_sem, r_sem, other_core)

    @pl.when(zh > 0)
    def _():
        far_wait()
        send_fields(0)

    pl.when(has_far)(from_far.wait_recv)
    quarter = ext[at_multiple(rim + core * (rows - rim), rim)]
    forward(1, quarter, at1[...], ext[at_multiple(start1, rows - rim)])

    @pl.when(zh == 0)
    def _():
        far_wait()
        send_fields(0)

    send_fields(1)

    pair = 1.0 / (members * (members - 1))

    def score(c):
        all_of(fq[c], len(meet), fq_s.at[c], fq_r.at[c]).wait_recv()
        step = 16
        for lo in range(0, share[c], step):
            f = [decoded(fq[c][m, lo : lo + step, :]) for m in range(members)]
            want = tall[at_multiple(base[c] + x * share[c] + lo, step)]
            weight = want[:, lanes - 1 :]
            want = jnp.where(lane < vars_n, want, 0.0)
            good = jnp.zeros_like(want)
            spread = jnp.zeros_like(want)
            pull = []
            for m in range(members):
                d = f[m] - want
                q = d * d + GAP
                root = lax.rsqrt(q)
                good = good + q * root
                pull.append((1.0 / members) * (d * root))
            for m in range(members):
                for n in range(m + 1, members):
                    d = f[m] - f[n]
                    q = d * d + GAP
                    root = lax.rsqrt(q)
                    spread = spread + q * root
                    slant = pair * (d * root)
                    pull[m] = pull[m] - slant
                    pull[n] = pull[n] + slant
            total = weight * (good * (1.0 / members) - pair * spread)
            lacc[...] += total[0:8] + total[8:16]
            for i in range(XN):
                mine = jnp.where(zh == 0, pull[i], pull[XN + i])
                gq[c][i, lo : lo + step, :] = (weight * mine).astype(BF16)

    def send_g(c):
        here = at_multiple(base[c] + x * share[c], share[c])
        for dx in range(1, XN):
            src = gq[c].at[(x + dx) % XN]
            remote(src, gs.at[here], gq_s.at[c], gq_r.at[c], to_x[dx - 1]).start()
        gs[here] = gq[c][x]

    def wait_g(c):
        all_of(gq[c], XN - 1, gq_s.at[c], gq_r.at[c]).wait_recv()

    def backward(c):
        here = pl.ds(base[c], size[c])
        grad_y = dot(gs[here], pv[...], 1, 0)
        grad_pre = (grad_y * slope[here]).astype(BF16)
        gx = dot(grad_pre, w[...], 1, 1) * gain[...]
        xh = unit[here]
        flat = jnp.mean(gx, axis=-1, keepdims=True)
        lean = jnp.mean(gx * xh, axis=-1, keepdims=True)
        gm = scale[here][:, 0:1] * (gx - flat - xh * lean)
        direct[here] = grad_y + gm
        gmb[here] = gm.astype(BF16)

    score(0)
    send_g(0)
    score(1)
    mine1 = x * YN + y
    lone[mine1] = jnp.where(lane < vars_n, jnp.sum(lacc[...], axis=0, keepdims=True), 0.0)
    for to in to_xy:
        remote(lone.at[mine1], lone.at[mine1], l1_s, l1_r, to).start()
    send_g(1)
    per = 1.0 / nb.shape[0]

    wait_g(1)
    backward(1)
    block = gmb[base[1] :]
    gsend[1] = (dot(at1[at_multiple(core * half, rim), :], block, 1, 0) * per).astype(BF16)
    grad_far = remote(gsend.at[1], garr.at[1], gh_s.at[1], gh_r.at[1], far)
    pl.when(has_far)(grad_far.start)

    wait_g(0)
    backward(0)
    wide = gmb[0 : size[0]]
    gsend[0] = (dot(at0[at_multiple((1 - core) * rows, rim), :], wide, 1, 0) * per).astype(BF16)
    grad_near = remote(gsend.at[0], garr.at[0], gh_s.at[0], gh_r.at[0], other_core)
    grad_near.start()

    loss_one = all_of(lone, len(to_xy), l1_s, l1_r)
    loss_one.wait_recv()
    mine2 = zl * CORES + core
    acc = lone[0]
    for i in range(1, XN * YN):
        acc = acc + lone[i]
    ltwo[mine2] = acc
    for to in [other_core] + to_zc:
        remote(ltwo.at[mine2], ltwo.at[mine2], l2_s, l2_r, to).start()

    tot[...] = dot(at0[at_multiple(core * rim, rows), :], wide, 1, 0) * per
    tot[rim : rim + half] += direct[0:half]
    tot[near_rows] += direct[half : half + rim]
    tot[at_multiple(core * half, half)] += dot(at1[at_multiple((1 - core) * rim, half), :], block, 1, 0) * per
    tot[far_rows] += direct[base[1] :]
    remote(garr.at[0], garr.at[0], gh_s.at[0], gh_r.at[0], other_core).wait_recv()
    tot[near_rows] += garr[0].astype(F32)
    out_ref[...] = tot[...].astype(BF16)

    @pl.when(has_far)
    def _():
        remote(garr.at[1], garr.at[1], gh_s.at[1], gh_r.at[1], far).wait_recv()
        out_ref[far_rows] = (tot[far_rows] + garr[1].astype(F32)).astype(BF16)

    loss_two = all_of(ltwo, 1 + len(to_zc), l2_s, l2_r)
    loss_two.wait_recv()
    acc = ltwo[0]
    for i in range(1, ZL * CORES):
        acc = acc + ltwo[i]
    loss = jnp.sum(acc, axis=-1, keepdims=True) * (1.0 / (total_points * vars_n))
    loss_ref[...] = jnp.broadcast_to(loss, loss_ref.shape)

    loss_one.wait_send()
    loss_two.wait_send()
    for c in range(2):
        all_of(fq[c], len(meet), fq_s.at[c], fq_r.at[c]).wait_send()
        all_of(gq[c], XN - 1, gq_s.at[c], gq_r.at[c]).wait_send()
    halo_near.wait_send()
    grad_near.wait_send()
    pl.when(has_far)(halo_far.wait_send)
    pl.when(has_far)(grad_far.wait_send)


def store(made, total, out_hbm, loss_hbm, one, sem):
    copy = pltpu.make_async_copy(made, out_hbm, sem.at[0])
    copy.start()
    one[...] = total[:, 0:1]
    small = pltpu.make_async_copy(one, loss_hbm, sem.at[1])
    small.start()
    copy.wait()
    small.wait()


def shards(
    latent_fields, neighbours, mix_weight, norm_gain, output_projector, verifying_fields, area
):
    _, rows, c_dim = latent_fields.shape
    count = neighbours.shape[0]
    vars_n = output_projector.shape[0]
    rim, lanes = rows // 4, 128
    members = ZH * XN
    anywhere = pl.BlockSpec(memory_space=pl.ANY)
    dma = pltpu.SemaphoreType.DMA
    n_xy, n_zc = XN * YN, ZL * CORES
    out, loss = pl.pallas_call(
        functools.partial(kernel, rows * lax.axis_size("grid")),
        out_shape=(
            pltpu.VMEM((rows, c_dim), BF16),
            pltpu.VMEM((1, lanes), F32),
        ),
        in_specs=[anywhere] * 7,
        out_specs=(
            pl.BlockSpec(memory_space=pltpu.VMEM),
            pl.BlockSpec(memory_space=pltpu.VMEM),
        ),
        scratch_shapes=[
            pltpu.VMEM((rows + 2 * rim, c_dim), BF16),
            pltpu.VMEM(mix_weight.shape, BF16),
            pltpu.VMEM((vars_n, c_dim), BF16),
            pltpu.VMEM((lanes, c_dim), BF16),
            pltpu.VMEM((count, rows), jnp.int32),
            pltpu.VMEM((1, c_dim), F32),
            pltpu.VMEM((vars_n, rows), F32),
            pltpu.VMEM((1, rows), F32),
            pltpu.VMEM((lanes, rows), F32),
            pltpu.VMEM((rows, lanes), F32),
            pltpu.VMEM((rows + rim, rows - rim), BF16),
            pltpu.VMEM((rows - rim, rim), BF16),
            pltpu.VMEM((rows, c_dim), F32),
            pltpu.VMEM((rows, lanes), F32),
            pltpu.VMEM((rows, c_dim), F32),
            pltpu.VMEM((rows, lanes), jnp.int16),
            pltpu.VMEM((members, (rows - rim) // XN, lanes), jnp.int16),
            pltpu.VMEM((members, rim // XN, lanes), jnp.int16),
            pltpu.VMEM((XN, (rows - rim) // XN, lanes), BF16),
            pltpu.VMEM((XN, rim // XN, lanes), BF16),
            pltpu.VMEM((rows, lanes), BF16),
            pltpu.VMEM((rows, c_dim), F32),
            pltpu.VMEM((rows, c_dim), BF16),
            pltpu.VMEM((rows, c_dim), F32),
            pltpu.VMEM((2, rim, c_dim), BF16),
            pltpu.VMEM((2, rim, c_dim), BF16),
            pltpu.VMEM((8, lanes), F32),
            pltpu.VMEM((n_xy, 1, lanes), F32),
            pltpu.VMEM((n_zc, 1, lanes), F32),
            pltpu.SemaphoreType.REGULAR,
            pltpu.SemaphoreType.REGULAR,
            dma((7,)),
            dma((2,)),
            dma((2,)),
            dma((2,)),
            dma((2,)),
            dma((2,)),
            dma((2,)),
            dma((2,)),
            dma((2,)),
            dma(()),
            dma(()),
            dma(()),
            dma(()),
        ],
        compiler_params=pltpu.CompilerParams(
            collective_id=0, has_side_effects=True, vmem_limit_bytes=63 << 20
        ),
        name="crps_layer",
    )(
        latent_fields.reshape(rows, c_dim),
        neighbours,
        mix_weight,
        norm_gain.reshape(1, c_dim),
        output_projector,
        verifying_fields,
        area.reshape(1, rows),
    )
    out, loss = pl.pallas_call(
        store,
        out_shape=(
            jax.ShapeDtypeStruct((rows, c_dim), BF16),
            jax.ShapeDtypeStruct((1, 1), F32),
        ),
        in_specs=[pl.BlockSpec(memory_space=pltpu.VMEM)] * 2,
        out_specs=(anywhere, anywhere),
        scratch_shapes=[pltpu.VMEM((1, 1), F32), dma((2,))],
        compiler_params=pltpu.CompilerParams(vmem_limit_bytes=16 << 20),
        name="store_result",
    )(out, loss)
    return (out[None], loss.reshape(()))


def solution(mesh):
    in_specs = (P("ens", "grid", None), P(None, "grid"), P(), P(), P(), P(None, "grid"), P("grid"))
    out_specs = (P("ens", "grid", None), P())
    return jax.shard_map(shards, mesh=mesh, in_specs=in_specs, out_specs=out_specs, check_vma=False)
```

```python
import functools

import jax
import jax.numpy as jnp
from jax import lax
from jax.experimental import pallas as pl
from jax.experimental.pallas import tpu as pltpu
from jax.sharding import PartitionSpec as P

ZH, XN, ZL, YN, CORES = 2, 4, 8, 4, 2
MESH = pl.DeviceIdType.MESH
GAP = 0.01
F32, BF16 = jnp.float32, jnp.bfloat16


def dot(a, b, ca, cb):
    return lax.dot_general(a, b, (((ca,), (cb,)), ((), ())), preferred_element_type=F32)


def device(zh, x, zl, y, core):
    return (zh * XN + x, (zl * YN + y) * CORES + core)


def kernel(
    total_points,
    x_hbm,
    nb_hbm,
    w_hbm,
    gain_hbm,
    proj_hbm,
    ver_hbm,
    area_hbm,
    out_ref,
    loss_ref,
    ext,
    w,
    pin,
    pv,
    nb,
    gain,
    ver,
    area,
    vert,
    tall,
    at0,
    at1,
    unit,
    scale,
    slope,
    fld,
    fq0,
    fq1,
    gq0,
    gq1,
    gs,
    direct,
    gmb,
    tot,
    gsend,
    garr,
    lacc,
    lone,
    ltwo,
    near_sem,
    far_sem,
    in_sem,
    halo_s,
    halo_r,
    fq_s,
    fq_r,
    gq_s,
    gq_r,
    gh_s,
    gh_r,
    l1_s,
    l1_r,
    l2_s,
    l2_r,
):
    rows, c_dim = x_hbm.shape
    rim = rows // 4
    half = rows // 2
    vars_n = proj_hbm.shape[0]
    lanes = pv.shape[0]
    members = ZH * XN
    e, g = lax.axis_index("ens"), lax.axis_index("grid")
    bands = lax.axis_size("grid")
    zh, x = e // XN, e % XN
    zl, y, core = g // (YN * CORES), (g // CORES) % YN, g % CORES
    chip, chips = g // CORES, bands // CORES
    first, last = chip == 0, chip == chips - 1
    upper = core == 1
    has_far = jnp.where(upper, jnp.logical_not(last), jnp.logical_not(first))
    far = (e, g - 1 + 2 * core)

    base, size = (0, rows - rim), (rows - rim, rim)
    share = tuple(n // XN for n in size)
    fq, gq = (fq0, fq1), (gq0, gq1)

    def at_multiple(start, n):
        return pl.ds(pl.multiple_of(start, 16), n)

    near_rows = at_multiple((1 - core) * (rows - rim), rim)
    far_rows = at_multiple(core * (rows - rim), rim)
    near_halo = at_multiple((1 - core) * (rows + rim), rim)
    far_halo = at_multiple(core * (rows + rim), rim)

    def at_z(d, core_):
        z = (zh * ZL + zl + d + ZH * ZL) % (ZH * ZL)
        return device(z // ZL, x, z % ZL, y, core_)

    offsets = [d for d in range(-(ZL // 2) + 1, ZL // 2 + 1) if d]
    xy = [(dx, dy) for dx in range(XN) for dy in range(YN) if (dx, dy) != (0, 0)]
    to_xyc = [device(zh, x, zl, y, 1 - core)] + [
        device(zh, (x + dx) % XN, zl, (y + dy) % YN, (core + dc) % CORES) for dx, dy in xy for dc in range(CORES)
    ]
    to_z = [at_z(d, core) for d in offsets]
    other_core = device(zh, x, zl, y, 1 - core)
    to_x = [device(zh, (x + dx) % XN, zl, y, core) for dx in range(1, XN)]
    meet = [(dh, dx) for dh in range(ZH - 1, -1, -1) for dx in range(XN) if (dh, dx) != (0, 0)]
    to_meet = [device((zh + dh) % ZH, (x + dx) % XN, zl, y, core) for dh, dx in meet]

    barrier = pltpu.get_barrier_semaphore()

    def hello(to):
        pl.semaphore_signal(barrier, inc=1, device_id=to, device_id_type=MESH)

    far_hellos = (
        [device(1 - zh, (x + dx) % XN, zl, y, 1) for dx in range(XN)]
        + [at_z(-d, 1) for d in offsets]
        + [device(zh, (x + dx) % XN, zl, (y + dy) % YN, 1) for dx, dy in xy]
    )

    @pl.when(upper)
    def _():
        hello((e, g - 1))
        pl.when(jnp.logical_not(last))(lambda: hello((e, g + 1)))

    @pl.when(jnp.logical_and(jnp.logical_not(upper), jnp.logical_not(first)))
    def _():
        hello((e, g - CORES))

    loads = [
        pltpu.make_async_copy(nb_hbm, nb, in_sem.at[0]),
        pltpu.make_async_copy(x_hbm, ext.at[pl.ds(rim, rows)], in_sem.at[1]),
        pltpu.make_async_copy(gain_hbm, gain, in_sem.at[2]),
        pltpu.make_async_copy(w_hbm, w, in_sem.at[3]),
        pltpu.make_async_copy(proj_hbm, pin, in_sem.at[4]),
        pltpu.make_async_copy(ver_hbm, ver, in_sem.at[5]),
        pltpu.make_async_copy(area_hbm, area, in_sem.at[6]),
    ]
    for load in loads:
        load.start()

    for to in far_hellos:
        hello(to)

    @pl.when(jnp.logical_not(has_far))
    def _():
        ext[far_halo] = jnp.zeros((rim, c_dim), BF16)

    def near_wait():
        @pl.when(jnp.logical_not(upper))
        def _():
            pl.semaphore_wait(barrier, 3 - first.astype(jnp.int32) - last.astype(jnp.int32))
            pl.semaphore_signal(near_sem, inc=1, device_id=other_core, device_id_type=MESH)

        @pl.when(upper)
        def _():
            pl.semaphore_wait(near_sem, 1)

    def far_wait():
        @pl.when(upper)
        def _():
            pl.semaphore_wait(barrier, CORES * len(far_hellos))
            pl.semaphore_signal(far_sem, inc=1, device_id=other_core, device_id_type=MESH)

        @pl.when(jnp.logical_not(upper))
        def _():
            pl.semaphore_wait(far_sem, 1)

    def remote(src, dst, s_sem, r_sem, to):
        return pltpu.make_async_remote_copy(
            src_ref=src, dst_ref=dst, send_sem=s_sem, recv_sem=r_sem, device_id=to, device_id_type=MESH
        )

    halo_near = remote(
        x_hbm.at[near_rows],
        ext.at[at_multiple(core * (rows + rim), rim)],
        halo_s.at[0],
        halo_r.at[0],
        other_core,
    )
    halo_far = remote(
        x_hbm.at[far_rows],
        ext.at[at_multiple((1 - core) * (rows + rim), rim)],
        halo_s.at[1],
        halo_r.at[1],
        far,
    )
    from_near = remote(ext.at[near_halo], ext.at[near_halo], halo_s.at[0], halo_r.at[0], other_core)
    from_far = remote(ext.at[far_halo], ext.at[far_halo], halo_s.at[1], halo_r.at[1], far)

    loads[0].wait()
    near = pltpu.roll(nb[...] - (g * rows - rim), rows - rim, axis=1)
    ends = near[:, half:]
    near = jnp.concatenate([near[:, :half], jnp.where(upper, pltpu.roll(ends, rim, axis=1), ends)], axis=1)
    start0 = (1 - core) * rim
    start1 = core * (rows - rim)

    def counts(start, height, lo, width):
        q = lax.broadcasted_iota(jnp.int32, (height, width), 0) + start
        total = jnp.zeros((height, width), F32)
        for k in range(nb.shape[0]):
            total = total + jnp.where(q == near[k : k + 1, lo : lo + width], 1.0, 0.0)
        return total.astype(BF16)

    at0[...] = counts(start0, rows + rim, 0, size[0])
    at1[...] = counts(start1, rows - rim, base[1], size[1])
    near_wait()
    halo_near.start()
    pl.when(has_far)(halo_far.start)

    def coded(f):
        most = jnp.max(jnp.abs(f), axis=-1, keepdims=True)
        power = jnp.ceil(jnp.log2(jnp.maximum(most, 1e-30)))
        code = jnp.where(lane < lanes - 1, jnp.round(f * jnp.exp2(14.0 - power)), power)
        return code.astype(jnp.int32).astype(jnp.int16)

    def decoded(code):
        f = code.astype(jnp.int32).astype(F32)
        return jnp.where(lane < vars_n, f * jnp.exp2(f[:, lanes - 1 :] - 14.0), 0.0)

    lane = lax.broadcasted_iota(jnp.int32, (1, lanes), 1)

    def forward(c, state, at, window):
        mixed = state.astype(F32) + dot(at, window, 0, 0) * (1.0 / nb.shape[0])
        centre = mixed - jnp.mean(mixed, axis=-1, keepdims=True)
        r = lax.rsqrt(jnp.mean(centre * centre, axis=-1, keepdims=True) + 1e-05)
        xh = centre * r
        here = pl.ds(base[c], size[c])
        unit[here] = xh
        scale[here] = jnp.broadcast_to(r, (size[c], scale.shape[1]))
        normed = (xh * gain[...]).astype(BF16)
        pre = dot(normed, w[...], 1, 0)
        k0 = 0.7978845608028654
        sq = pre * pre
        t = jnp.tanh(k0 * pre * (1.0 + 0.044715 * sq))
        cdf = 0.5 * (1.0 + t)
        out = (state.astype(F32) + pre * cdf).astype(BF16)
        slope[here] = cdf + 0.5 * pre * (1.0 - t * t) * (k0 * (1.0 + 3 * 0.044715 * sq))
        fld[here] = coded(dot(out, pv[...], 1, 1))
        fq[c][e] = fld[at_multiple(base[c] + x * share[c], share[c])]

    loads[1].wait()
    loads[2].wait()
    loads[3].wait()
    loads[4].wait()
    pv[0 : vars_n // 16 * 16] = pin[0 : vars_n // 16 * 16]
    pv[vars_n // 16 * 16 :] = jnp.zeros((lanes - vars_n // 16 * 16, c_dim), BF16)
    pv[vars_n // 16 * 16 : vars_n] = pin[vars_n // 16 * 16 :]
    from_near.wait_recv()
    quarter = ext[at_multiple(rim + (1 - core) * (rows - rim), rim)]
    state = jnp.concatenate([ext[2 * rim : 2 * rim + half], quarter], axis=0)
    forward(0, state, at0[...], ext[at_multiple(start0, rows + rim)])

    loads[5].wait()
    loads[6].wait()
    vert[0:vars_n] = ver[...]
    vert[vars_n:] = jnp.broadcast_to(area[...], (lanes - vars_n, rows))
    turned = pltpu.roll(vert[...], rows - rim, axis=1).T
    tall[0:half] = turned[0:half]
    tall[at_multiple(half + core * rim, rim)] = turned[half : half + rim]
    tall[at_multiple(half + (1 - core) * rim, rim)] = turned[half + rim :]
    lacc[...] = jnp.zeros(lacc.shape, F32)

    def shared(c, i):
        (dh, dx), to = meet[i], to_meet[i]
        there = at_multiple(base[c] + ((x + dx) % XN) * share[c], share[c])
        return remote(fld.at[there], fq[c].at[e], fq_s.at[c], fq_r.at[c], to)

    def send_fields(c):
        for i in range(len(meet)):
            shared(c, i).start()

    def all_of(ref, count, s_sem, r_sem):
        some = ref.at[pl.ds(0, count)]
        return remote(some, some, s_sem, r_sem, other_core)

    @pl.when(zh > 0)
    def _():
        far_wait()
        send_fields(0)

    pl.when(has_far)(from_far.wait_recv)
    quarter = ext[at_multiple(rim + core * (rows - rim), rim)]
    forward(1, quarter, at1[...], ext[at_multiple(start1, rows - rim)])

    @pl.when(zh == 0)
    def _():
        far_wait()
        send_fields(0)

    send_fields(1)

    pair = 1.0 / (members * (members - 1))

    def score(c):
        all_of(fq[c], len(meet), fq_s.at[c], fq_r.at[c]).wait_recv()
        step = 16
        for lo in range(0, share[c], step):
            f = [decoded(fq[c][m, lo : lo + step, :]) for m in range(members)]
            want = tall[at_multiple(base[c] + x * share[c] + lo, step)]
            weight = want[:, lanes - 1 :]
            want = jnp.where(lane < vars_n, want, 0.0)
            good = jnp.zeros_like(want)
            spread = jnp.zeros_like(want)
            pull = []
            for m in range(members):
                d = f[m] - want
                q = d * d + GAP
                root = lax.rsqrt(q)
                good = good + q * root
                pull.append((1.0 / members) * (d * root))
            for m in range(members):
                for n in range(m + 1, members):
                    d = f[m] - f[n]
                    q = d * d + GAP
                    root = lax.rsqrt(q)
                    spread = spread + q * root
                    slant = pair * (d * root)
                    pull[m] = pull[m] - slant
                    pull[n] = pull[n] + slant
            total = weight * (good * (1.0 / members) - pair * spread)
            lacc[...] += total[0:8] + total[8:16]
            for i in range(XN):
                mine = jnp.where(zh == 0, pull[i], pull[XN + i])
                gq[c][i, lo : lo + step, :] = (weight * mine).astype(BF16)

    def send_g(c):
        here = at_multiple(base[c] + x * share[c], share[c])
        for dx in range(1, XN):
            src = gq[c].at[(x + dx) % XN]
            remote(src, gs.at[here], gq_s.at[c], gq_r.at[c], to_x[dx - 1]).start()
        gs[here] = gq[c][x]

    def wait_g(c):
        all_of(gq[c], XN - 1, gq_s.at[c], gq_r.at[c]).wait_recv()

    def backward(c):
        here = pl.ds(base[c], size[c])
        grad_y = dot(gs[here], pv[...], 1, 0)
        grad_pre = (grad_y * slope[here]).astype(BF16)
        gx = dot(grad_pre, w[...], 1, 1) * gain[...]
        xh = unit[here]
        flat = jnp.mean(gx, axis=-1, keepdims=True)
        lean = jnp.mean(gx * xh, axis=-1, keepdims=True)
        gm = scale[here][:, 0:1] * (gx - flat - xh * lean)
        direct[here] = grad_y + gm
        gmb[here] = gm.astype(BF16)

    score(0)
    send_g(0)
    score(1)
    mine1 = (x * YN + y) * CORES + core
    lone[mine1] = jnp.where(lane < vars_n, jnp.sum(lacc[...], axis=0, keepdims=True), 0.0)
    for to in to_xyc:
        remote(lone.at[mine1], lone.at[mine1], l1_s, l1_r, to).start()
    send_g(1)
    per = 1.0 / nb.shape[0]

    wait_g(1)
    backward(1)
    block = gmb[base[1] :]
    gsend[1] = (dot(at1[at_multiple(core * half, rim), :], block, 1, 0) * per).astype(BF16)
    grad_far = remote(gsend.at[1], garr.at[1], gh_s.at[1], gh_r.at[1], far)
    pl.when(has_far)(grad_far.start)

    wait_g(0)
    backward(0)
    wide = gmb[0 : size[0]]
    gsend[0] = (dot(at0[at_multiple((1 - core) * rows, rim), :], wide, 1, 0) * per).astype(BF16)
    grad_near = remote(gsend.at[0], garr.at[0], gh_s.at[0], gh_r.at[0], other_core)
    grad_near.start()

    loss_one = all_of(lone, len(to_xyc), l1_s, l1_r)
    loss_one.wait_recv()
    mine2 = zl
    acc = lone[0]
    for i in range(1, XN * YN * CORES):
        acc = acc + lone[i]
    ltwo[mine2] = acc
    for to in to_z:
        remote(ltwo.at[mine2], ltwo.at[mine2], l2_s, l2_r, to).start()

    tot[...] = dot(at0[at_multiple(core * rim, rows), :], wide, 1, 0) * per
    tot[rim : rim + half] += direct[0:half]
    tot[near_rows] += direct[half : half + rim]
    tot[at_multiple(core * half, half)] += dot(at1[at_multiple((1 - core) * rim, half), :], block, 1, 0) * per
    tot[far_rows] += direct[base[1] :]
    remote(garr.at[0], garr.at[0], gh_s.at[0], gh_r.at[0], other_core).wait_recv()
    tot[near_rows] += garr[0].astype(F32)
    out_ref[...] = tot[...].astype(BF16)

    @pl.when(has_far)
    def _():
        remote(garr.at[1], garr.at[1], gh_s.at[1], gh_r.at[1], far).wait_recv()
        out_ref[far_rows] = (tot[far_rows] + garr[1].astype(F32)).astype(BF16)

    loss_two = all_of(ltwo, len(to_z), l2_s, l2_r)
    loss_two.wait_recv()
    acc = ltwo[0]
    for i in range(1, ZL):
        acc = acc + ltwo[i]
    loss = jnp.sum(acc, axis=-1, keepdims=True) * (1.0 / (total_points * vars_n))
    loss_ref[...] = jnp.broadcast_to(loss, loss_ref.shape)

    loss_one.wait_send()
    loss_two.wait_send()
    for c in range(2):
        all_of(fq[c], len(meet), fq_s.at[c], fq_r.at[c]).wait_send()
        all_of(gq[c], XN - 1, gq_s.at[c], gq_r.at[c]).wait_send()
    halo_near.wait_send()
    grad_near.wait_send()
    pl.when(has_far)(halo_far.wait_send)
    pl.when(has_far)(grad_far.wait_send)


def store(made, total, out_hbm, loss_hbm, one, sem):
    copy = pltpu.make_async_copy(made, out_hbm, sem.at[0])
    copy.start()
    one[...] = total[:, 0:1]
    small = pltpu.make_async_copy(one, loss_hbm, sem.at[1])
    small.start()
    copy.wait()
    small.wait()


def shards(
    latent_fields, neighbours, mix_weight, norm_gain, output_projector, verifying_fields, area
):
    _, rows, c_dim = latent_fields.shape
    count = neighbours.shape[0]
    vars_n = output_projector.shape[0]
    rim, lanes = rows // 4, 128
    members = ZH * XN
    anywhere = pl.BlockSpec(memory_space=pl.ANY)
    dma = pltpu.SemaphoreType.DMA
    n_xyc, n_z = XN * YN * CORES, ZL
    out, loss = pl.pallas_call(
        functools.partial(kernel, rows * lax.axis_size("grid")),
        out_shape=(
            pltpu.VMEM((rows, c_dim), BF16),
            pltpu.VMEM((1, lanes), F32),
        ),
        in_specs=[anywhere] * 7,
        out_specs=(
            pl.BlockSpec(memory_space=pltpu.VMEM),
            pl.BlockSpec(memory_space=pltpu.VMEM),
        ),
        scratch_shapes=[
            pltpu.VMEM((rows + 2 * rim, c_dim), BF16),
            pltpu.VMEM(mix_weight.shape, BF16),
            pltpu.VMEM((vars_n, c_dim), BF16),
            pltpu.VMEM((lanes, c_dim), BF16),
            pltpu.VMEM((count, rows), jnp.int32),
            pltpu.VMEM((1, c_dim), F32),
            pltpu.VMEM((vars_n, rows), F32),
            pltpu.VMEM((1, rows), F32),
            pltpu.VMEM((lanes, rows), F32),
            pltpu.VMEM((rows, lanes), F32),
            pltpu.VMEM((rows + rim, rows - rim), BF16),
            pltpu.VMEM((rows - rim, rim), BF16),
            pltpu.VMEM((rows, c_dim), F32),
            pltpu.VMEM((rows, lanes), F32),
            pltpu.VMEM((rows, c_dim), F32),
            pltpu.VMEM((rows, lanes), jnp.int16),
            pltpu.VMEM((members, (rows - rim) // XN, lanes), jnp.int16),
            pltpu.VMEM((members, rim // XN, lanes), jnp.int16),
            pltpu.VMEM((XN, (rows - rim) // XN, lanes), BF16),
            pltpu.VMEM((XN, rim // XN, lanes), BF16),
            pltpu.VMEM((rows, lanes), BF16),
            pltpu.VMEM((rows, c_dim), F32),
            pltpu.VMEM((rows, c_dim), BF16),
            pltpu.VMEM((rows, c_dim), F32),
            pltpu.VMEM((2, rim, c_dim), BF16),
            pltpu.VMEM((2, rim, c_dim), BF16),
            pltpu.VMEM((8, lanes), F32),
            pltpu.VMEM((n_xyc, 1, lanes), F32),
            pltpu.VMEM((n_z, 1, lanes), F32),
            pltpu.SemaphoreType.REGULAR,
            pltpu.SemaphoreType.REGULAR,
            dma((7,)),
            dma((2,)),
            dma((2,)),
            dma((2,)),
            dma((2,)),
            dma((2,)),
            dma((2,)),
            dma((2,)),
            dma((2,)),
            dma(()),
            dma(()),
            dma(()),
            dma(()),
        ],
        compiler_params=pltpu.CompilerParams(
            collective_id=0, has_side_effects=True, vmem_limit_bytes=63 << 20
        ),
        name="crps_layer",
    )(
        latent_fields.reshape(rows, c_dim),
        neighbours,
        mix_weight,
        norm_gain.reshape(1, c_dim),
        output_projector,
        verifying_fields,
        area.reshape(1, rows),
    )
    out, loss = pl.pallas_call(
        store,
        out_shape=(
            jax.ShapeDtypeStruct((rows, c_dim), BF16),
            jax.ShapeDtypeStruct((1, 1), F32),
        ),
        in_specs=[pl.BlockSpec(memory_space=pltpu.VMEM)] * 2,
        out_specs=(anywhere, anywhere),
        scratch_shapes=[pltpu.VMEM((1, 1), F32), dma((2,))],
        compiler_params=pltpu.CompilerParams(vmem_limit_bytes=16 << 20),
        name="store_result",
    )(out, loss)
    return (out[None], loss.reshape(()))


def solution(mesh):
    in_specs = (P("ens", "grid", None), P(None, "grid"), P(), P(), P(), P(None, "grid"), P("grid"))
    out_specs = (P("ens", "grid", None), P())
    return jax.shard_map(shards, mesh=mesh, in_specs=in_specs, out_specs=out_specs, check_vma=False)
```
